256 devices in a mesh: grp: 8 (over z), seq: 32 (over x, y, core).
Axes of the slice: x: 4, y: 4, z: 8, core: 2. Of those that a mesh axis runs over, the one named last changes fastest.
Arguments:
- q_proj: bfloat16 [4096, 32768], P(None, ('grp', 'seq')), may hold values from -8 to 8
- k_proj: bfloat16 [4096, 32768], P(None, ('grp', 'seq')), may hold values from -8 to 8
- v_proj: bfloat16 [4096, 32768], P(None, ('grp', 'seq')), may hold values from -6 to 6
- block_start: int32 [256], replicated, may hold values from 0 to 128, as said below
- kv_select: int32 [256, 3], P(('grp', 'seq')), may hold values from 0 to 1, as said below
- pre_gate: bfloat16 [4096, 32768], P(None, ('grp', 'seq')), may hold values from -6 to 6
- post_gate: bfloat16 [4096, 32768], P(None, ('grp', 'seq')), may hold values from -6 to 6
- long_filter: bfloat16 [4096, 32768], P(('grp', 'seq')), may hold values from -1.5 to 1.5
Outputs:
- attn_out: bfloat16 [4096, 32768], P(None, ('grp', 'seq'))
- mixed: bfloat16 [4096, 32768], P(None, ('grp', 'seq'))
The draws below stay inside these ranges and needn't reach their ends.
Inputs may be any that keep to these rules, and one draw needn't show every extreme that they name: `block_start`: A record begins at that offset of the block; 128 means that none begins in it. At most one record begins in a block. `kv_select`: column j is 1 where the block reads the keys and values of the block j + 1 places before it. Only blocks at or after the start of the record of the block's first token are read, none before the first block, and the block itself begins no record at offset 0 where any flag is set. Some block reads all 3.
All inputs are finite; a program needn't handle non-finite values.
Results may differ from the reference program's by a relative error of at most 0.0065.
Values may be sent and summed in bfloat16 or wider, within the bound.
No kernel may reach another device: no remote copies, remote signals or barrier semaphores. Data moves between devices by JAX's collectives and lax.ppermute only.
A program may use at most 128 MiB of HBM per device.

```python
import math
import jax
import jax.numpy as jnp
from jax import lax

HEADS = 32
HD = 128
CHANNEL_COUNT = 4096
TOK = 128
W = 3
NBLK = 256
SEQUENCE_LENGTH = 32768


def record_plan(key):
    key_offset = jax.random.fold_in(key, 101)
    key_opened = jax.random.fold_in(key, 102)
    key_coin = jax.random.fold_in(key, 103)
    key_anchor = jax.random.fold_in(key, 104)
    offset = jax.random.randint(key_offset, (NBLK,), 0, TOK)
    opened = jax.random.randint(key_opened, (NBLK,), 0, 5) == 0
    anchor = jax.random.randint(key_anchor, (), W, NBLK)
    block_ids = jnp.arange(NBLK, dtype=jnp.int32)
    quiet_zone = (block_ids > anchor - W) & (block_ids <= anchor)
    opened = opened & jnp.logical_not(quiet_zone)
    block_start = jnp.where(opened, offset, TOK).astype(jnp.int32)
    counted = jnp.cumsum(opened.astype(jnp.int32))
    target = block_ids[:, None]
    source = target - jnp.arange(1, W + 1, dtype=jnp.int32)[None, :]
    between = counted[jnp.maximum(target - 1, 0)] - counted[jnp.maximum(source, 0)]
    eligible = (source >= 0) & (between == 0) & (block_start[:, None] != 0)
    coin_flip = jax.random.randint(key_coin, (NBLK, W), 0, 2) == 1
    chosen = eligible & (coin_flip | (target == anchor))
    return (block_start, chosen.astype(jnp.int32))


def draw_block_start(key, part):
    return record_plan(key)[0]


def draw_kv_select(key, part):
    return record_plan(key)[1]


def draw_q_proj(key, part):
    key = jax.random.fold_in(key, 11)
    drawn_draw = jnp.clip(1.6 * jax.random.normal(key, (CHANNEL_COUNT, SEQUENCE_LENGTH), jnp.float32), -8.0, 8.0)
    return drawn_draw.astype(jnp.bfloat16)


def draw_k_proj(key, part):
    key = jax.random.fold_in(key, 12)
    drawn_draw = jnp.clip(1.6 * jax.random.normal(key, (CHANNEL_COUNT, SEQUENCE_LENGTH), jnp.float32), -8.0, 8.0)
    return drawn_draw.astype(jnp.bfloat16)


def draw_long_filter(key, part):
    key = jax.random.fold_in(key, 31)
    key_memory = jax.random.fold_in(key, 1)
    key_runs = jax.random.fold_in(key, 2)
    key_noise = jax.random.fold_in(key, 3)
    fraction = jax.random.uniform(key_memory, (CHANNEL_COUNT, 1), jnp.float32)
    low = math.log(30.0)
    noise_draw = jnp.clip(jax.random.normal(key_noise, (CHANNEL_COUNT, SEQUENCE_LENGTH), jnp.float32), -5.0, 5.0)
    high = math.log(4.0 * SEQUENCE_LENGTH)
    memory = jnp.exp(low + fraction * (high - low))
    token_positions = jnp.arange(SEQUENCE_LENGTH, dtype=jnp.int32)[None, :]
    query_runs = jax.random.randint(key_runs, (CHANNEL_COUNT, 3), 0, SEQUENCE_LENGTH)
    passed_through = (token_positions >= query_runs[:, 0:1]).astype(jnp.float32)
    passed_through = passed_through + (token_positions >= query_runs[:, 1:2]).astype(jnp.float32)
    passed_through = passed_through + (token_positions >= query_runs[:, 2:3]).astype(jnp.float32)
    amplitude = jnp.sqrt(2.0 / memory)
    decay = jnp.exp(-token_positions.astype(jnp.float32) / memory)
    return (noise_draw * amplitude * decay * jnp.power(0.6, passed_through)).astype(jnp.bfloat16)


def steps_of(rng, extent, cuts, smallest, high):
    loudness, own = 1.0, jax.random.fold_in(rng, 6)
    for position, shards_of in cuts:
        draws = jnp.exp(jax.random.uniform(jax.random.fold_in(own, position), (shards_of,), jnp.float32, smallest / len(cuts), high / len(cuts)))
        loudness = loudness * jnp.repeat(draws, extent[position] // shards_of).reshape([-1 if axis == position else 1 for axis in range(len(extent))])
    return loudness


def noise(own_key, dims, scale, bound, pieces=(), held_as=jnp.bfloat16):
    result = scale * jax.random.normal(own_key, dims, jnp.float32)
    if pieces:
        result = result * steps_of(own_key, dims, pieces, -0.22, 0.18)
    return jnp.clip(result, -bound, bound).astype(held_as)


def setup_inputs(seed: int = 0) -> dict:
    keys = jax.random.split(jax.random.key(seed), 9)
    q_proj = draw_q_proj(jax.random.fold_in(keys[8], 71), 0)
    k_proj = draw_k_proj(jax.random.fold_in(keys[8], 71), 0)
    v_proj = noise(keys[2], (CHANNEL_COUNT, SEQUENCE_LENGTH), 1.0, 6.0, ((1, 256),))
    block_start = draw_block_start(jax.random.fold_in(keys[8], 71), 0)
    kv_select = draw_kv_select(jax.random.fold_in(keys[8], 71), 0)
    pre_gate = noise(keys[5], (CHANNEL_COUNT, SEQUENCE_LENGTH), 1.0, 6.0, ((1, 256),))
    post_gate = noise(keys[6], (CHANNEL_COUNT, SEQUENCE_LENGTH), 1.0, 6.0, ((1, 256),))
    long_filter = draw_long_filter(jax.random.fold_in(keys[8], 71), 0)
    return {"q_proj": q_proj, "k_proj": k_proj, "v_proj": v_proj, "block_start": block_start, "kv_select": kv_select, "pre_gate": pre_gate, "post_gate": post_gate, "long_filter": long_filter}


def record_ids(block_start):
    opened = (block_start < TOK).astype(jnp.int32)
    before = jnp.cumsum(opened) - opened
    within = jnp.arange(TOK, dtype=jnp.int32)
    return before[:, None] + (within[None, :] >= block_start[:, None]).astype(jnp.int32)

def attend_block(block_index, q_proj, keys_pad, values_pad, record_pad, kv_select):
    queries = lax.dynamic_slice_in_dim(q_proj, block_index * TOK, TOK, 1)
    key_rows = lax.dynamic_slice_in_dim(keys_pad, block_index * TOK, (W + 1) * TOK, 1)
    key_rows = key_rows.reshape(CHANNEL_COUNT, W + 1, TOK)[:, ::-1]
    value_rows = lax.dynamic_slice_in_dim(values_pad, block_index * TOK, (W + 1) * TOK, 1)
    value_rows = value_rows.reshape(CHANNEL_COUNT, W + 1, TOK)[:, ::-1]
    record = lax.dynamic_slice_in_dim(record_pad, block_index, W + 1, 0)[::-1]
    chosen = lax.dynamic_slice_in_dim(kv_select, block_index, 1, 0)[0]
    allowed = jnp.concatenate([jnp.ones((1,), jnp.int32), chosen]) == 1
    query_f = queries.reshape(HEADS, HD, TOK).astype(jnp.float32)
    key_f = key_rows.reshape(HEADS, HD, W + 1, TOK).astype(jnp.float32)
    value_f = value_rows.reshape(HEADS, HD, W + 1, TOK).astype(jnp.float32)
    scores = jnp.einsum('hdq,hdrk->hqrk', query_f, key_f) / math.sqrt(HD)
    lanes = jnp.arange(TOK, dtype=jnp.int32)
    same_record = record[0][:, None, None] == record[None, :, :]
    causal = lanes[None, None, :] <= lanes[:, None, None]
    is_own = (jnp.arange(W + 1) == 0)[None, :, None]
    visible = same_record & jnp.where(is_own, causal, allowed[None, :, None])
    masked = jnp.where(visible[None], scores, -jnp.inf)
    row_top = lax.optimization_barrier(jnp.max(masked, axis=(2, 3), keepdims=True))
    weights = jnp.where(visible[None], jnp.exp(masked - row_top), 0.0)
    denominator = lax.optimization_barrier(jnp.sum(weights, axis=(2, 3)))
    rounded = lax.optimization_barrier(weights.astype(jnp.bfloat16)).astype(jnp.float32)
    weighted = jnp.einsum('hqrk,hdrk->hdq', rounded, value_f)
    return (weighted / denominator[:, None, :]).astype(jnp.bfloat16).reshape(CHANNEL_COUNT, TOK)

def convolve(pair):
    signal, kernel = pair
    spectrum = jnp.fft.rfft(signal, n=2 * SEQUENCE_LENGTH, axis=-1) * jnp.fft.rfft(kernel, n=2 * SEQUENCE_LENGTH, axis=-1)
    return jnp.fft.irfft(spectrum, n=2 * SEQUENCE_LENGTH, axis=-1)[:, :SEQUENCE_LENGTH]

def reference(q_proj, k_proj, v_proj, block_start, kv_select, pre_gate, post_gate, long_filter):
    padding = ((0, 0), (W * TOK, 0))
    keys_pad = jnp.pad(k_proj, padding)
    values_pad = jnp.pad(v_proj, padding)
    record_pad = jnp.concatenate([-jnp.ones((W, TOK), jnp.int32), record_ids(block_start)], 0)
    blocks = lax.map(lambda block_index: attend_block(block_index, q_proj, keys_pad, values_pad, record_pad, kv_select), jnp.arange(NBLK, dtype=jnp.int32))
    attn_out = blocks.transpose(1, 0, 2).reshape(CHANNEL_COUNT, SEQUENCE_LENGTH)
    attn_f = lax.optimization_barrier(attn_out).astype(jnp.float32)
    mixed_in = (attn_f * pre_gate.astype(jnp.float32)).astype(jnp.bfloat16)
    group_size = math.gcd(CHANNEL_COUNT, 256)
    signal = mixed_in.astype(jnp.float32).reshape(CHANNEL_COUNT // group_size, group_size, SEQUENCE_LENGTH)
    kernel = long_filter.astype(jnp.float32).reshape(CHANNEL_COUNT // group_size, group_size, SEQUENCE_LENGTH)
    conv_full = lax.map(convolve, (signal, kernel)).reshape(CHANNEL_COUNT, SEQUENCE_LENGTH)
    conv_out = lax.optimization_barrier(conv_full.astype(jnp.bfloat16)).astype(jnp.float32)
    mixed = (post_gate.astype(jnp.float32) * conv_out).astype(jnp.bfloat16)
    return (attn_out, mixed)
```

```python
import math

import jax
import jax.numpy as jnp
import ml_dtypes
import numpy as np
from jax import lax
from jax.experimental import pallas as pl
from jax.experimental.pallas import tpu as pltpu
from jax.sharding import Mesh
from jax.sharding import PartitionSpec as P

HD = 128
ALL = ("z", "x", "y", "c")
MASKED = -1e30
VMEM_LIMIT = 48 * 1024 * 1024


def hi_lo(table):
    high = table.astype(ml_dtypes.bfloat16)
    low = (table - high.astype(np.float64)).astype(ml_dtypes.bfloat16)
    return (high, low)


def make_tables(rows, width):
    length = rows * width
    k1 = np.arange(rows)[:, None]
    n1 = np.arange(rows)[None, :]
    theta = 2.0 * np.pi * (((4 * k1 + 1) * n1) % (4 * rows)) / (4 * rows)
    n2 = np.arange(width)[None, :]
    turn = 2.0 * np.pi * (((4 * k1 + 1) * n2) % (4 * length)) / (4 * length)
    k2 = np.arange(width)[:, None]
    phi = 2.0 * np.pi * ((k2 * n2) % width) / width
    first = hi_lo(np.concatenate([np.cos(theta), -np.sin(theta)], axis=0))
    second = hi_lo(np.block([[np.cos(phi), -np.sin(phi)], [np.sin(phi), np.cos(phi)]]))
    second_back = hi_lo(np.block([[np.cos(phi), np.sin(phi)], [-np.sin(phi), np.cos(phi)]]))
    first_back = hi_lo(np.concatenate([np.cos(theta).T, -np.sin(theta).T], axis=1) / length)
    twist = (np.cos(turn).astype(np.float32), -np.sin(turn).astype(np.float32))
    return first, twist, second, second_back, first_back


def dot(left, right):
    return jnp.dot(left, right, preferred_element_type=jnp.float32)


def split(value):
    high = value.astype(jnp.bfloat16)
    low = (value - high.astype(jnp.float32)).astype(jnp.bfloat16)
    return high, low


def forward(signal, first_h, first_l, cosine, sine, second_h, second_l):
    rows = signal.shape[0]
    width = signal.shape[1] // 2
    part = dot(first_h, signal) + dot(first_l, signal)
    turned = []
    for channel in range(2):
        lanes = slice(channel * width, (channel + 1) * width)
        real, imag = part[:rows, lanes], part[rows:, lanes]
        turned.append(
            jnp.concatenate([real * cosine - imag * sine, real * sine + imag * cosine], axis=1)
        )
    high, low = split(jnp.concatenate(turned, axis=0))
    return dot(high, second_h) + (dot(low, second_h) + dot(high, second_l))


def filter_kernel(filter_ref, first_h, first_l, cosine, sine, second_h, second_l, out_ref):
    out_ref[...] = forward(
        filter_ref[...], first_h[...], first_l[...], cosine[...], sine[...], second_h[...], second_l[...]
    )


def conv_kernel(
    signal_ref,
    spectrum_ref,
    first_h,
    first_l,
    cosine_ref,
    sine_ref,
    second_h,
    second_l,
    second_back_h,
    second_back_l,
    first_back_h,
    first_back_l,
    out_ref,
):
    rows = signal_ref.shape[0]
    width = signal_ref.shape[1] // 2
    cosine, sine = cosine_ref[...], sine_ref[...]
    spectrum = forward(
        signal_ref[...], first_h[...], first_l[...], cosine, sine, second_h[...], second_l[...]
    )
    other = spectrum_ref[...]
    real, imag = spectrum[:, :width], spectrum[:, width:]
    other_real, other_imag = other[:, :width], other[:, width:]
    product = jnp.concatenate(
        [real * other_real - imag * other_imag, real * other_imag + imag * other_real], axis=1
    )
    high, low = split(product)
    table = second_back_h[...]
    part = dot(high, table) + (dot(low, table) + dot(high, second_back_l[...]))
    reals, imags = [], []
    for channel in range(2):
        block = part[channel * rows : (channel + 1) * rows]
        real, imag = block[:, :width], block[:, width:]
        reals.append(real * cosine + imag * sine)
        imags.append(imag * cosine - real * sine)
    turned = jnp.concatenate(
        [jnp.concatenate(reals, axis=1), jnp.concatenate(imags, axis=1)], axis=0
    )
    high, low = split(turned)
    table = first_back_h[...]
    result = dot(table, high) + (dot(table, low) + dot(first_back_l[...], high))
    out_ref[...] = result.astype(jnp.bfloat16)


def whole(array):
    return pl.BlockSpec(array.shape, lambda step: (0,) * array.ndim)


def transform_filter(taps, tables):
    first, twist, second, _, _ = tables
    rows, lanes = taps.shape
    width = twist[0].shape[1]
    pairs = lanes // (2 * width)
    constants = [jnp.asarray(entry) for entry in (*first, *twist, *second)]
    return pl.pallas_call(
        filter_kernel,
        grid=(pairs,),
        in_specs=[pl.BlockSpec((rows, 2 * width), lambda step: (0, step))]
        + [whole(entry) for entry in constants],
        out_specs=pl.BlockSpec((2 * rows, 2 * width), lambda step: (step, 0)),
        out_shape=jax.ShapeDtypeStruct((2 * pairs * rows, 2 * width), jnp.float32),
        compiler_params=pltpu.CompilerParams(vmem_limit_bytes=VMEM_LIMIT),
        cost_estimate=pl.CostEstimate(
            flops=2 * pairs * 170_000_000, bytes_accessed=6 * 1024 * 1024, transcendentals=0
        ),
        name="filter_spectrum",
    )(taps, *constants)


def convolve(signal, spectrum, tables):
    first, twist, second, second_back, first_back = tables
    rows, lanes = signal.shape
    width = twist[0].shape[1]
    pairs = lanes // (2 * width)
    constants = [
        jnp.asarray(entry) for entry in (*first, *twist, *second, *second_back, *first_back)
    ]
    return pl.pallas_call(
        conv_kernel,
        grid=(pairs,),
        in_specs=[
            pl.BlockSpec((rows, 2 * width), lambda step: (0, step)),
            pl.BlockSpec((2 * rows, 2 * width), lambda step: (step, 0)),
        ]
        + [whole(entry) for entry in constants],
        out_specs=pl.BlockSpec((rows, 2 * width), lambda step: (0, step)),
        out_shape=jax.ShapeDtypeStruct(signal.shape, jnp.bfloat16),
        compiler_params=pltpu.CompilerParams(vmem_limit_bytes=VMEM_LIMIT),
        cost_estimate=pl.CostEstimate(
            flops=2 * pairs * 370_000_000, bytes_accessed=8 * 1024 * 1024, transcendentals=0
        ),
        name="convolve",
    )(signal, spectrum, *constants)


def attend_kernel(bias_ref, q_ref, k_own, v_own, k_near, v_near, k_far, v_far, out_ref):
    heads = q_ref.shape[1] // HD
    for head in range(heads):
        rows = slice(head * HD, (head + 1) * HD)
        queries = jnp.concatenate([q_ref[0, rows], q_ref[1, rows]], axis=1)
        keys = jnp.concatenate(
            [k_far[rows], k_near[0, rows], k_near[1, rows], k_own[0, rows], k_own[1, rows]], axis=1
        )
        scores = lax.dot_general(
            keys, queries, (((0,), (0,)), ((), ())), preferred_element_type=jnp.float32
        )
        masked = scores * (1.0 / math.sqrt(HD)) + bias_ref[...]
        weights = jnp.exp(masked - jnp.max(masked, axis=0, keepdims=True))
        total = jnp.sum(weights, axis=0, keepdims=True)
        values = jnp.concatenate(
            [v_far[rows], v_near[0, rows], v_near[1, rows], v_own[0, rows], v_own[1, rows]], axis=1
        )
        mixed = (dot(values, weights.astype(jnp.bfloat16)) / total).astype(jnp.bfloat16)
        tokens = q_ref.shape[2]
        out_ref[0, rows] = mixed[:, :tokens]
        out_ref[1, rows] = mixed[:, tokens:]


def attend(bias, q_own, k_own, v_own, k_near, v_near, k_far, v_far, step_heads=4):
    channels, tokens = q_own.shape[1:]
    step_rows = step_heads * HD
    pair = pl.BlockSpec((2, step_rows, tokens), lambda step: (0, step, 0))
    single = pl.BlockSpec((step_rows, tokens), lambda step: (step, 0))
    return pl.pallas_call(
        attend_kernel,
        grid=(channels // step_rows,),
        in_specs=[whole(bias), pair, pair, pair, pair, pair, single, single],
        out_specs=pair,
        out_shape=jax.ShapeDtypeStruct(q_own.shape, jnp.bfloat16),
        compiler_params=pltpu.CompilerParams(vmem_limit_bytes=VMEM_LIMIT),
        cost_estimate=pl.CostEstimate(
            flops=(channels // HD) * 4 * HD * 640 * 256,
            bytes_accessed=6 * 1024 * 1024,
            transcendentals=(channels // HD) * 640 * 256,
        ),
        name="attend",
    )(bias, q_own, k_own, v_own, k_near, v_near, k_far, v_far)


def chip_bias(block_start, flags, chip, reach, tokens):
    first = 2 * chip
    key_ids = first - reach + jnp.arange(reach + 2, dtype=jnp.int32)
    opened = (block_start < tokens).astype(jnp.int32)
    all_ids = jnp.arange(block_start.shape[0], dtype=jnp.int32)
    base = jnp.sum(jnp.where(all_ids[None, :] < key_ids[:, None], opened[None, :], 0), axis=1)
    start = jnp.sum(jnp.where(all_ids[None, :] == key_ids[:, None], block_start[None, :], 0), axis=1)
    lanes = jnp.arange(tokens, dtype=jnp.int32)
    record = base[:, None] + (lanes[None, :] >= start[:, None]).astype(jnp.int32)
    same = record[:, :, None, None] == record[None, None, reach:, :]
    causal = lanes[None, :, None, None] <= lanes[None, None, None, :]
    distance = (reach + jnp.arange(2))[None, :] - jnp.arange(reach + 2)[:, None]
    picked = jnp.zeros((reach + 2, 2), jnp.int32)
    for step in range(1, reach + 1):
        picked = jnp.where(distance == step, flags[None, :, step - 1], picked)
    earlier = ((picked == 1) & (key_ids[:, None] >= 0))[:, None, :, None]
    own = (distance == 0)[:, None, :, None]
    visible = same & (earlier | (own & causal))
    bias = jnp.where(visible, 0.0, MASKED).astype(jnp.float32)
    return bias.reshape((reach + 2) * tokens, 2 * tokens)


def over_cores(value):
    return lax.all_to_all(value, "c", split_axis=0, concat_axis=0, tiled=True)


def next_chip(value):
    count = math.prod(lax.axis_size(name) for name in ALL)
    return lax.ppermute(value, ALL, [(source, (source + 2) % count) for source in range(count)])


def body(q_proj, k_proj, v_proj, block_start, kv_select, pre_gate, post_gate, long_filter):
    channels, tokens = q_proj.shape
    devices = math.prod(lax.axis_size(name) for name in ALL)
    reach = kv_select.shape[1]
    own = channels // devices
    half = channels // 2
    tables = make_tables(devices, tokens)

    k_own = over_cores(k_proj.reshape(2, half, tokens))
    k_near = next_chip(k_own)
    v_own = over_cores(v_proj.reshape(2, half, tokens))
    v_near = next_chip(v_own)
    k_far = next_chip(k_near[1])
    v_far = next_chip(v_near[1])
    q_own = over_cores(q_proj.reshape(2, half, tokens))

    flags = lax.all_gather(kv_select.astype(jnp.float32), "c", axis=0, tiled=True).astype(jnp.int32)
    chip = lax.axis_index(("z", "x", "y"))
    bias = chip_bias(block_start, flags, chip, reach, tokens)

    taps = long_filter.reshape(own, devices, tokens).transpose(1, 0, 2).reshape(devices, own * tokens)
    spectrum = transform_filter(taps, tables)

    halves = attend(bias, q_own, k_own, v_own, k_near, v_near, k_far, v_far)
    attn_out = over_cores(halves).reshape(channels, tokens)
    mixed_in = (attn_out.astype(jnp.float32) * pre_gate.astype(jnp.float32)).astype(jnp.bfloat16)

    gathered = lax.all_to_all(
        mixed_in.reshape(devices, own, tokens), ALL, split_axis=0, concat_axis=0, tiled=True
    )
    conv_out = convolve(gathered.reshape(devices, own * tokens), spectrum, tables)
    returned = lax.all_to_all(
        conv_out.reshape(devices, own, tokens), ALL, split_axis=0, concat_axis=0, tiled=True
    ).reshape(channels, tokens)
    mixed = (post_gate.astype(jnp.float32) * returned.astype(jnp.float32)).astype(jnp.bfloat16)
    return (attn_out, mixed)


def solution(mesh):
    chips = Mesh(mesh.devices.reshape(8, 4, 4, 2), ALL)
    return jax.shard_map(
        body,
        mesh=chips,
        in_specs=(
            P(None, ALL),
            P(None, ALL),
            P(None, ALL),
            P(),
            P(ALL, None),
            P(None, ALL),
            P(None, ALL),
            P(ALL, None),
        ),
        out_specs=(P(None, ALL), P(None, ALL)),
        check_vma=False,
    )
```

```python
import math

import jax
import jax.numpy as jnp
import ml_dtypes
import numpy as np
from jax import lax
from jax.experimental import pallas as pl
from jax.experimental.pallas import tpu as pltpu
from jax.sharding import Mesh
from jax.sharding import PartitionSpec as P

HD = 128
ALL = ("za", "zb", "zc", "x", "y", "c")
CHIPS = ("za", "zb", "x", "y", "zc")
OWNERS = ("za", "zb", "c", "x", "y", "zc")
STEPS = 4
MASKED = -1e30
VMEM_LIMIT = 48 * 1024 * 1024
HBM_ONLY = 60 * 1024 * 1024


def hi_lo(table):
    high = table.astype(ml_dtypes.bfloat16)
    low = (table - high.astype(np.float64)).astype(ml_dtypes.bfloat16)
    return (high, low)


def make_tables(rows, width):
    length = rows * width
    k1 = np.arange(rows)[:, None]
    n1 = np.arange(rows)[None, :]
    theta = 2.0 * np.pi * (((4 * k1 + 1) * n1) % (4 * rows)) / (4 * rows)
    n2 = np.arange(width)[None, :]
    turn = 2.0 * np.pi * (((4 * k1 + 1) * n2) % (4 * length)) / (4 * length)
    k2 = np.arange(width)[:, None]
    phi = 2.0 * np.pi * ((k2 * n2) % width) / width
    first = hi_lo(np.concatenate([np.cos(theta), -np.sin(theta)], axis=0))
    second = hi_lo(np.block([[np.cos(phi), -np.sin(phi)], [np.sin(phi), np.cos(phi)]]))
    second_back = hi_lo(np.block([[np.cos(phi), np.sin(phi)], [-np.sin(phi), np.cos(phi)]]))
    first_back = hi_lo(np.concatenate([np.cos(theta).T, -np.sin(theta).T], axis=1) / length)
    twist = (np.cos(turn).astype(np.float32), -np.sin(turn).astype(np.float32))
    blocks = np.arange(rows).reshape(4, 2, -1, 2)
    arriving = blocks.transpose(0, 2, 1, 3).reshape(-1)
    leaving = blocks.transpose(0, 3, 2, 1).reshape(-1)
    first_moved = np.concatenate([table[:, arriving] for table in first], axis=1)
    first = np.concatenate(first, axis=1)
    second = np.concatenate([second[0], second[0], second[1]], axis=0)
    second_back = np.concatenate([second_back[0], second_back[0], second_back[1]], axis=0)
    high, low = (table[leaving] for table in first_back)
    first_back = np.concatenate([high, high, low], axis=1)
    return first, first_moved, twist, second, second_back, first_back


def dot(left, right):
    return jnp.dot(left, right, preferred_element_type=jnp.float32)


def split(value):
    high = value.astype(jnp.bfloat16)
    low = (value - high.astype(jnp.float32)).astype(jnp.bfloat16)
    return high, low


def turned_by(real, imag, cosine, sine):
    return real * cosine - imag * sine, real * sine + imag * cosine


def forward(signals, first, cosine, sine, second):
    rows, width = signals[0].shape
    signal = jnp.concatenate(signals, axis=1)
    part = dot(first, jnp.concatenate([signal, signal], axis=0))
    turned = []
    for channel in range(2):
        lanes = slice(channel * width, (channel + 1) * width)
        turned.append(
            jnp.concatenate(turned_by(part[:rows, lanes], part[rows:, lanes], cosine, sine), axis=1)
        )
    high, low = split(jnp.concatenate(turned, axis=0))
    return dot(jnp.concatenate([high, low, high], axis=1), second)


def filter_kernel(filter_ref, first, cosine, sine, second, out_ref):
    for pair in range(filter_ref.shape[0] // 2):
        signals = [filter_ref[2 * pair], filter_ref[2 * pair + 1]]
        rows = signals[0].shape[0]
        out_ref[2 * rows * pair : 2 * rows * (pair + 1)] = forward(
            signals, first[...], cosine[...], sine[...], second[...]
        )


def conv_kernel(
    signal_ref, spectrum_ref, first, cosine_ref, sine_ref, second, second_back, first_back, out_ref
):
    rows, width = signal_ref.shape[1:]
    cosine, sine = cosine_ref[...], sine_ref[...]
    for pair in range(signal_ref.shape[0] // 2):
        signals = [signal_ref[2 * pair], signal_ref[2 * pair + 1]]
        spectrum = forward(signals, first[...], cosine, sine, second[...])
        other = spectrum_ref[2 * rows * pair : 2 * rows * (pair + 1)]
        product = jnp.concatenate(
            turned_by(spectrum[:, :width], spectrum[:, width:], other[:, :width], other[:, width:]),
            axis=1,
        )
        high, low = split(product)
        part = dot(jnp.concatenate([high, low, high], axis=1), second_back[...])
        reals, imags = [], []
        for channel in range(2):
            block = part[channel * rows : (channel + 1) * rows]
            real, imag = turned_by(block[:, :width], block[:, width:], cosine, -sine)
            reals.append(real)
            imags.append(imag)
        turned = jnp.concatenate(
            [jnp.concatenate(reals, axis=1), jnp.concatenate(imags, axis=1)], axis=0
        )
        high, low = split(turned)
        result = dot(first_back[...], jnp.concatenate([high, low, high], axis=0))
        result = result.astype(jnp.bfloat16)
        out_ref[2 * pair] = result[:, :width]
        out_ref[2 * pair + 1] = result[:, width:]


def whole(array):
    return pl.BlockSpec(array.shape, lambda step: (0,) * array.ndim)


def transform_filter(taps, tables, step_channels=4):
    first, _, twist, second, _, _ = tables
    channels, rows, width = taps.shape
    constants = [jnp.asarray(entry) for entry in (first, *twist, second)]
    return pl.pallas_call(
        filter_kernel,
        grid=(channels // step_channels,),
        in_specs=[pl.BlockSpec((step_channels, rows, width), lambda step: (step, 0, 0))]
        + [whole(entry) for entry in constants],
        out_specs=pl.BlockSpec((step_channels * rows, 2 * width), lambda step: (step, 0)),
        out_shape=jax.ShapeDtypeStruct((channels * rows, 2 * width), jnp.float32),
        compiler_params=pltpu.CompilerParams(vmem_limit_bytes=VMEM_LIMIT),
        cost_estimate=pl.CostEstimate(
            flops=channels * 170_000_000, bytes_accessed=6 * 1024 * 1024, transcendentals=0
        ),
        name="filter_spectrum",
    )(taps, *constants)


def convolve(signal, spectrum, tables, step_channels=4):
    _, first, twist, second, second_back, first_back = tables
    channels, rows, width = signal.shape
    constants = [jnp.asarray(entry) for entry in (first, *twist, second, second_back, first_back)]
    block = pl.BlockSpec((step_channels, rows, width), lambda step: (step, 0, 0))
    return pl.pallas_call(
        conv_kernel,
        grid=(channels // step_channels,),
        in_specs=[
            block,
            pl.BlockSpec((step_channels * rows, 2 * width), lambda step: (step, 0)),
        ]
        + [whole(entry) for entry in constants],
        out_specs=block,
        out_shape=jax.ShapeDtypeStruct(signal.shape, jnp.bfloat16),
        compiler_params=pltpu.CompilerParams(vmem_limit_bytes=VMEM_LIMIT),
        cost_estimate=pl.CostEstimate(
            flops=channels * 370_000_000, bytes_accessed=8 * 1024 * 1024, transcendentals=0
        ),
        name="convolve",
    )(signal, spectrum, *constants)


def pick_heads(which, first, second):
    tokens = first.shape[1]
    pairs = [value.reshape(STEPS, 2, -1, tokens) for value in (first, second)]
    return jnp.stack(
        [
            lax.dynamic_index_in_dim(pair, which, 1, keepdims=False).reshape(-1, tokens)
            for pair in pairs
        ]
    )


def attend_kernel(
    core_ref,
    bias_ref,
    q_mine,
    gate_mine,
    q_other,
    gate_other,
    far,
    near,
    crossed,
    own,
    sibling,
    out_mine,
    out_other,
    gated,
):
    heads, tokens = q_mine.shape[0] // HD, q_mine.shape[1]
    group = gated.shape[2]
    core = core_ref[0]
    pairs = (far, near, crossed, own, sibling)
    for head in range(heads):
        rows = slice(head * HD, (head + 1) * HD)
        queries = jnp.concatenate([q_mine[rows], q_other[rows]], axis=1)
        keys = jnp.concatenate([pair[0, rows] for pair in pairs], axis=1)
        scores = lax.dot_general(
            keys, queries, (((0,), (0,)), ((), ())), preferred_element_type=jnp.float32
        )
        masked = scores * (math.log2(math.e) / math.sqrt(HD)) + bias_ref[...]
        weights = jnp.exp2(masked - jnp.max(masked, axis=0, keepdims=True))
        total = jnp.sum(weights, axis=0, keepdims=True)
        values = jnp.concatenate([pair[1, rows] for pair in pairs], axis=1)
        mixed = (dot(values, weights.astype(jnp.bfloat16)) / total).astype(jnp.bfloat16)
        gates = ((out_mine, gate_mine, core), (out_other, gate_other, 1 - core))
        for place, (out, gate, block) in enumerate(gates):
            part = mixed[:, place * tokens : (place + 1) * tokens]
            out[rows] = part
            product = (part.astype(jnp.float32) * gate[rows].astype(jnp.float32)).astype(jnp.bfloat16)
            owners = slice(head * HD // group, (head + 1) * HD // group)
            gated[owners, block] = product.reshape(HD // group, group, tokens)


def attend(core, bias, q_proj, gate, exchanged, blocks, group):
    channels, tokens = q_proj.shape[0] // 2, q_proj.shape[1]
    step_rows = channels // STEPS
    half = pl.BlockSpec((step_rows, tokens), lambda step, core: (2 * step + core[0], 0))
    single = pl.BlockSpec((step_rows, tokens), lambda step, core: (step, 0))
    pair = pl.BlockSpec((2, step_rows, tokens), lambda step, core: (0, step, 0))
    pieces = [
        pl.BlockSpec((None, step_rows, tokens), lambda step, core, which=which: (which, step, 0))
        for which in range(2)
    ]
    return pl.pallas_call(
        attend_kernel,
        grid_spec=pltpu.PrefetchScalarGridSpec(
            num_scalar_prefetch=1,
            grid=(STEPS,),
            in_specs=[pl.BlockSpec(bias.shape, lambda step, core: (0, 0)), half, half, *pieces]
            + [pair] * 5,
            out_specs=[
                single,
                single,
                pl.BlockSpec((step_rows // group, 2, group, tokens), lambda step, core: (step, 0, 0, 0)),
            ],
        ),
        out_shape=[
            jax.ShapeDtypeStruct((channels, tokens), jnp.bfloat16),
            jax.ShapeDtypeStruct((channels, tokens), jnp.bfloat16),
            jax.ShapeDtypeStruct((channels // group, 2, group, tokens), jnp.bfloat16),
        ],
        compiler_params=pltpu.CompilerParams(vmem_limit_bytes=HBM_ONLY),
        cost_estimate=pl.CostEstimate(
            flops=(channels // HD) * 4 * HD * bias.size,
            bytes_accessed=18 * 2 * channels * tokens + 4 * bias.size,
            transcendentals=(channels // HD) * bias.size,
        ),
        name="attend",
    )(core.reshape(1), bias, q_proj, gate, exchanged, exchanged, *blocks)


def chip_bias(block_start, flags, key_ids, query_ids, tokens):
    opened = (block_start < tokens).astype(jnp.int32)
    all_ids = jnp.arange(block_start.shape[0], dtype=jnp.int32)
    lanes = jnp.arange(tokens, dtype=jnp.int32)

    def records(ids):
        base = jnp.sum(jnp.where(all_ids[None, :] < ids[:, None], opened[None, :], 0), axis=1)
        start = jnp.sum(
            jnp.where(all_ids[None, :] == ids[:, None], block_start[None, :], 0), axis=1
        )
        return base[:, None] + (lanes[None, :] >= start[:, None]).astype(jnp.int32)

    same = records(key_ids)[:, :, None, None] == records(query_ids)[None, None, :, :]
    causal = lanes[None, :, None, None] <= lanes[None, None, None, :]
    distance = query_ids[None, :] - key_ids[:, None]
    picked = jnp.zeros(distance.shape, jnp.int32)
    for step in range(flags.shape[1]):
        picked = jnp.where(distance == step + 1, flags[None, :, step], picked)
    earlier = ((picked == 1) & (key_ids[:, None] >= 0))[:, None, :, None]
    own = (distance == 0)[:, None, :, None]
    visible = same & (earlier | (own & causal))
    bias = jnp.where(visible, 0.0, MASKED).astype(jnp.float32)
    return bias.reshape(key_ids.shape[0] * tokens, query_ids.shape[0] * tokens)


def devices_of():
    return math.prod(lax.axis_size(name) for name in ALL)


def send(value, target):
    count = devices_of()
    return lax.ppermute(value, ALL, [(source, target(source) % count) for source in range(count)])


def next_chip(value):
    return send(value, lambda source: source + 2)


def next_chip_crossed(value):
    return send(value, lambda source: (source + 2) ^ 1)


def second_next_chip(value):
    count, ring = devices_of(), lax.axis_size("y")

    def between(source):
        y = source // 2 % ring
        return source + 2 * ((y - 1) % ring - y)

    value = lax.ppermute(value, "y", [(y, (y - 1) % ring) for y in range(ring)])
    return lax.ppermute(
        value, ALL, [(between(source), (source + 4) % count) for source in range(count)]
    )


def to_sibling(value):
    return lax.ppermute(value, "c", [(0, 1), (1, 0)])


def body(q_proj, k_proj, v_proj, block_start, kv_select, pre_gate, post_gate, long_filter):
    channels, tokens = q_proj.shape
    devices = devices_of()
    group = channels // devices
    tables = make_tables(devices, tokens)
    core = lax.axis_index("c")
    first_core = core == 0

    other = pick_heads(1 - core, k_proj, v_proj)
    sibling = to_sibling(other)
    crossed = next_chip_crossed(other)
    k_later, v_later, other = lax.optimization_barrier((k_proj, v_proj, other))
    mine = pick_heads(core, k_later, v_later)
    near = next_chip(mine)
    odd = jnp.where(first_core, sibling, mine)
    far = second_next_chip(odd)
    flags = kv_select.astype(jnp.float32)
    flags = jnp.concatenate([flags, to_sibling(flags)], axis=0).astype(jnp.int32)
    first = 2 * lax.axis_index(ALL[:-1])
    key_ids = jnp.stack(
        [first - 3, first - 2 + core, first - 1 - core, first + core, first + 1 - core]
    )
    query_ids = jnp.stack([first + core, first + 1 - core])
    bias = chip_bias(block_start, flags, key_ids, query_ids, tokens)

    q_later, gate_later, bias, _ = lax.optimization_barrier((q_proj, pre_gate, bias, odd))
    exchanged_half = to_sibling(pick_heads(1 - core, q_later, gate_later))

    def exchanged(source):
        upper, zc, lower, c = source // 64, source // 32 % 2, source // 2 % 16, source % 2
        return upper * 64 + c * 32 + lower * 2 + zc

    taps = long_filter.reshape(group, devices, tokens)
    taps, bias, _ = lax.optimization_barrier((taps, bias, odd))
    taps, far, near = lax.optimization_barrier((taps, far, near))
    moved = [(source, exchanged(source)) for source in range(devices) if exchanged(source) != source]
    swapped = lax.ppermute(taps, ALL, moved)

    out_mine, out_other, gated = attend(
        core, bias, q_proj, pre_gate, exchanged_half, (far, near, crossed, mine, sibling), group
    )
    gated, swapped = lax.optimization_barrier((gated, swapped))
    taps = jnp.where(lax.axis_index("zc") == core, taps, swapped)
    spectrum = transform_filter(taps, tables)
    gathered = lax.all_to_all(gated, CHIPS, split_axis=0, concat_axis=0, tiled=True)
    out_other = to_sibling(out_other)
    attn_out = jnp.stack(
        [
            jnp.where(first_core, out_mine, out_other).reshape(STEPS, -1, tokens),
            jnp.where(first_core, out_other, out_mine).reshape(STEPS, -1, tokens),
        ],
        axis=1,
    ).reshape(channels, tokens)

    signal = gathered.reshape(devices, group, tokens).transpose(1, 0, 2)
    conv_out = convolve(signal, spectrum, tables).transpose(1, 0, 2)
    returned = lax.all_to_all(
        conv_out, OWNERS, split_axis=0, concat_axis=0, tiled=True
    ).reshape(channels, tokens)
    mixed = (post_gate.astype(jnp.float32) * returned.astype(jnp.float32)).astype(jnp.bfloat16)
    return (attn_out, mixed)


def solution(mesh):
    chips = Mesh(mesh.devices.reshape(2, 2, 2, 4, 4, 2), ALL)
    return jax.shard_map(
        body,
        mesh=chips,
        in_specs=(
            P(None, ALL),
            P(None, ALL),
            P(None, ALL),
            P(),
            P(ALL, None),
            P(None, ALL),
            P(None, ALL),
            P(ALL, None),
        ),
        out_specs=(P(None, ALL), P(None, ALL)),
        check_vma=False,
    )
```

```python
import math

import jax
import jax.numpy as jnp
import ml_dtypes
import numpy as np
from jax import lax
from jax.experimental import pallas as pl
from jax.experimental.pallas import tpu as pltpu
from jax.sharding import Mesh
from jax.sharding import PartitionSpec as P

HD = 128
ALL = ("za", "zb", "zc", "x", "y", "c")
CHIPS = ("za", "zb", "x", "y", "zc")
OWNERS = ("za", "zb", "c", "x", "y", "zc")
STEPS = 4
MASKED = -1e30
VMEM_LIMIT = 48 * 1024 * 1024
HBM_ONLY = 60 * 1024 * 1024


def hi_lo(table):
    high = table.astype(ml_dtypes.bfloat16)
    low = (table - high.astype(np.float64)).astype(ml_dtypes.bfloat16)
    return (high, low)


def make_tables(rows, width):
    length = rows * width
    k1 = np.arange(rows)[:, None]
    n1 = np.arange(rows)[None, :]
    theta = 2.0 * np.pi * (((4 * k1 + 1) * n1) % (4 * rows)) / (4 * rows)
    n2 = np.arange(width)[None, :]
    turn = 2.0 * np.pi * (((4 * k1 + 1) * n2) % (4 * length)) / (4 * length)
    k2 = np.arange(width)[:, None]
    phi = 2.0 * np.pi * ((k2 * n2) % width) / width
    first = hi_lo(np.concatenate([np.cos(theta), -np.sin(theta)], axis=0))
    second = hi_lo(np.block([[np.cos(phi), -np.sin(phi)], [np.sin(phi), np.cos(phi)]]))
    second_back = hi_lo(np.block([[np.cos(phi), np.sin(phi)], [-np.sin(phi), np.cos(phi)]]))
    first_back = hi_lo(np.concatenate([np.cos(theta).T, -np.sin(theta).T], axis=1) / length)
    twist = (np.cos(turn).astype(np.float32), -np.sin(turn).astype(np.float32))
    blocks = np.arange(rows).reshape(4, 2, -1, 2)
    arriving = blocks.transpose(0, 2, 1, 3).reshape(-1)
    leaving = blocks.transpose(0, 3, 2, 1).reshape(-1)
    first_moved = np.concatenate([table[:, arriving] for table in first], axis=1)
    first = np.concatenate(first, axis=1)
    second = np.concatenate([second[0], second[0], second[1]], axis=0)
    second_back = np.concatenate([second_back[0], second_back[0], second_back[1]], axis=0)
    high, low = (table[leaving] for table in first_back)
    first_back = np.concatenate([high, high, low], axis=1)
    return first, first_moved, twist, second, second_back, first_back


def dot(left, right):
    return jnp.dot(left, right, preferred_element_type=jnp.float32)


def split(value):
    high = value.astype(jnp.bfloat16)
    low = (value - high.astype(jnp.float32)).astype(jnp.bfloat16)
    return high, low


def turned_by(real, imag, cosine, sine):
    return real * cosine - imag * sine, real * sine + imag * cosine


def interleaved(tasks, lag=1):
    waiting, active, turn = list(tasks), [], 0
    while waiting or active:
        if waiting and turn % lag == 0:
            active.append(waiting.pop(0))
        active = [task for task in active if next(task, None) is not None]
        turn += 1


def forward(signals, first, cosine, sine, second):
    rows, width = signals[0].shape
    signal = jnp.concatenate(signals, axis=1)
    part = dot(first, jnp.concatenate([signal, signal], axis=0))
    yield part
    turned = []
    for channel in range(2):
        lanes = slice(channel * width, (channel + 1) * width)
        turned.append(
            jnp.concatenate(turned_by(part[:rows, lanes], part[rows:, lanes], cosine, sine), axis=1)
        )
    high, low = split(jnp.concatenate(turned, axis=0))
    yield dot(jnp.concatenate([high, low, high], axis=1), second)


def filter_task(pair, filter_ref, first, cosine, sine, second, out_ref):
    signals = [filter_ref[2 * pair], filter_ref[2 * pair + 1]]
    rows = signals[0].shape[0]
    for spectrum in forward(signals, first[...], cosine[...], sine[...], second[...]):
        yield True
    out_ref[2 * rows * pair : 2 * rows * (pair + 1)] = spectrum


def filter_kernel(filter_ref, *rest):
    pairs = filter_ref.shape[0] // 2
    interleaved([filter_task(pair, filter_ref, *rest) for pair in range(pairs)])


def conv_task(
    channel, place, rows, load, store, spectrum_ref, first, cosine_ref, sine_ref, second, second_back, first_back
):
    width = cosine_ref.shape[1]
    cosine, sine = cosine_ref[...], sine_ref[...]
    signals = [load(channel), load(channel + 1)]
    for spectrum in forward(signals, first[...], cosine, sine, second[...]):
        yield True
    other = spectrum_ref[rows * place : rows * (place + 2)]
    product = jnp.concatenate(
        turned_by(spectrum[:, :width], spectrum[:, width:], other[:, :width], other[:, width:]),
        axis=1,
    )
    high, low = split(product)
    part = dot(jnp.concatenate([high, low, high], axis=1), second_back[...])
    yield True
    reals, imags = [], []
    for half in range(2):
        block = part[half * rows : (half + 1) * rows]
        real, imag = turned_by(block[:, :width], block[:, width:], cosine, -sine)
        reals.append(real)
        imags.append(imag)
    turned = jnp.concatenate(
        [jnp.concatenate(reals, axis=1), jnp.concatenate(imags, axis=1)], axis=0
    )
    high, low = split(turned)
    result = dot(first_back[...], jnp.concatenate([high, low, high], axis=0))
    yield True
    store(channel, result[:, :width])
    store(channel + 1, result[:, width:])


def conv_kernel(signal_ref, spectrum_ref, *rest):
    *tables, out_ref, taken, given = rest
    rows, channels, width = signal_ref.shape
    here = spectrum_ref.shape[0] // rows
    step = pl.program_id(0)
    base = step * here

    @pl.when(step == 0)
    def _():
        taken[...] = signal_ref[...].astype(jnp.float32).reshape(taken.shape)

    def load(channel):
        return taken[pl.ds(base + channel, rows, stride=channels), :].astype(jnp.bfloat16)

    def store(channel, value):
        given[pl.ds(base + channel, rows, stride=channels), :] = value

    interleaved(
        [
            conv_task(channel, channel, rows, load, store, spectrum_ref, *tables)
            for channel in range(0, here, 2)
        ]
    )

    @pl.when(step == pl.num_programs(0) - 1)
    def _():
        out_ref[...] = given[...].reshape(out_ref.shape).astype(jnp.bfloat16)


def whole(array):
    return pl.BlockSpec(array.shape, lambda step: (0,) * array.ndim)


def transform_filter(taps, tables, step_channels=4):
    first, _, twist, second, _, _ = tables
    channels, rows, width = taps.shape
    constants = [jnp.asarray(entry) for entry in (first, *twist, second)]
    return pl.pallas_call(
        filter_kernel,
        grid=(channels // step_channels,),
        in_specs=[pl.BlockSpec((step_channels, rows, width), lambda step: (step, 0, 0))]
        + [whole(entry) for entry in constants],
        out_specs=pl.BlockSpec((step_channels * rows, 2 * width), lambda step: (step, 0)),
        out_shape=jax.ShapeDtypeStruct((channels * rows, 2 * width), jnp.float32),
        compiler_params=pltpu.CompilerParams(vmem_limit_bytes=VMEM_LIMIT),
        cost_estimate=pl.CostEstimate(
            flops=channels * 170_000_000, bytes_accessed=6 * 1024 * 1024, transcendentals=0
        ),
        name="filter_spectrum",
    )(taps, *constants)


def convolve(signal, spectrum, tables, step_channels=8):
    _, first, twist, second, second_back, first_back = tables
    rows, channels, width = signal.shape
    constants = [jnp.asarray(entry) for entry in (first, *twist, second, second_back, first_back)]
    return pl.pallas_call(
        conv_kernel,
        grid=(channels // step_channels,),
        in_specs=[
            whole(signal),
            pl.BlockSpec((step_channels * rows, 2 * width), lambda step: (step, 0)),
        ]
        + [whole(entry) for entry in constants],
        out_specs=whole(signal),
        out_shape=jax.ShapeDtypeStruct(signal.shape, jnp.bfloat16),
        scratch_shapes=[pltpu.VMEM((rows * channels, width), jnp.float32)] * 2,
        compiler_params=pltpu.CompilerParams(vmem_limit_bytes=VMEM_LIMIT),
        cost_estimate=pl.CostEstimate(
            flops=channels * 370_000_000, bytes_accessed=8 * 1024 * 1024, transcendentals=0
        ),
        name="convolve",
    )(signal, spectrum, *constants)


def pick_heads(which, first, second):
    tokens = first.shape[1]
    pairs = [value.reshape(STEPS, 2, -1, tokens) for value in (first, second)]
    return jnp.stack(
        [
            lax.dynamic_index_in_dim(pair, which, 1, keepdims=False).reshape(-1, tokens)
            for pair in pairs
        ]
    )


def attend_kernel(
    core_ref,
    bias_ref,
    q_mine,
    gate_mine,
    q_other,
    gate_other,
    far,
    near,
    crossed,
    own,
    sibling,
    out_mine,
    out_other,
    gated,
):
    heads, tokens = gate_other.shape[0] // HD, gate_other.shape[1]
    group = gated.shape[2]
    core = core_ref[0]
    pairs = (far, near, crossed, own, sibling)
    part_heads = q_mine.shape[1] // HD

    def rows_of(head):
        return slice(head * HD, (head + 1) * HD)

    def own_rows(ref, head):
        return ref[head // part_heads, rows_of(head % part_heads)]

    def task(head):
        rows = rows_of(head)
        queries = jnp.concatenate([own_rows(q_mine, head), q_other[rows]], axis=1)
        keys = jnp.concatenate([pair[0, rows] for pair in pairs], axis=1)
        scores = lax.dot_general(
            keys, queries, (((0,), (0,)), ((), ())), preferred_element_type=jnp.float32
        )
        yield True
        masked = scores * (math.log2(math.e) / math.sqrt(HD)) + bias_ref[...]
        weights = jnp.exp2(masked - jnp.max(masked, axis=0, keepdims=True))
        total = jnp.sum(weights, axis=0, keepdims=True)
        weights = weights.astype(jnp.bfloat16)
        yield True
        values = jnp.concatenate([pair[1, rows] for pair in pairs], axis=1)
        mixed = (dot(values, weights) * (1.0 / total)).astype(jnp.bfloat16)
        gates = (
            (out_mine, own_rows(gate_mine, head), core),
            (out_other, gate_other[rows], 1 - core),
        )
        for place, (out, gate, block) in enumerate(gates):
            part = mixed[:, place * tokens : (place + 1) * tokens]
            out[rows] = part
            product = (part.astype(jnp.float32) * gate.astype(jnp.float32)).astype(jnp.bfloat16)
            owners = slice(head * HD // group, (head + 1) * HD // group)
            gated[owners, block] = product.reshape(HD // group, group, tokens)

    interleaved([task(head) for head in range(heads)])


def attend(core, bias, q_proj, gate, exchanged, blocks, group, steps=2):
    channels, tokens = q_proj.shape[0] // 2, q_proj.shape[1]
    step_rows = channels // steps
    halves = [value.reshape(STEPS, 2, channels // STEPS, tokens) for value in (q_proj, gate)]
    half = pl.BlockSpec(
        (STEPS // steps, None, channels // STEPS, tokens), lambda step, core: (step, core[0], 0, 0)
    )
    single = pl.BlockSpec((step_rows, tokens), lambda step, core: (step, 0))
    pair = pl.BlockSpec((2, step_rows, tokens), lambda step, core: (0, step, 0))
    pieces = [
        pl.BlockSpec((None, step_rows, tokens), lambda step, core, which=which: (which, step, 0))
        for which in range(2)
    ]
    return pl.pallas_call(
        attend_kernel,
        grid_spec=pltpu.PrefetchScalarGridSpec(
            num_scalar_prefetch=1,
            grid=(steps,),
            in_specs=[pl.BlockSpec(bias.shape, lambda step, core: (0, 0)), half, half, *pieces]
            + [pair] * 5,
            out_specs=[
                single,
                single,
                pl.BlockSpec((step_rows // group, 2, group, tokens), lambda step, core: (step, 0, 0, 0)),
            ],
        ),
        out_shape=[
            jax.ShapeDtypeStruct((channels, tokens), jnp.bfloat16),
            jax.ShapeDtypeStruct((channels, tokens), jnp.bfloat16),
            jax.ShapeDtypeStruct((channels // group, 2, group, tokens), jnp.bfloat16),
        ],
        compiler_params=pltpu.CompilerParams(vmem_limit_bytes=HBM_ONLY),
        cost_estimate=pl.CostEstimate(
            flops=(channels // HD) * 4 * HD * bias.size,
            bytes_accessed=18 * 2 * channels * tokens + 4 * bias.size,
            transcendentals=(channels // HD) * bias.size,
        ),
        name="attend",
    )(core.reshape(1), bias, *halves, exchanged, exchanged, *blocks)


def chip_bias(block_start, flags, key_ids, query_ids, tokens):
    opened = (block_start < tokens).astype(jnp.int32)
    all_ids = jnp.arange(block_start.shape[0], dtype=jnp.int32)
    lanes = jnp.arange(tokens, dtype=jnp.int32)

    def records(ids):
        base = jnp.sum(jnp.where(all_ids[None, :] < ids[:, None], opened[None, :], 0), axis=1)
        start = jnp.sum(
            jnp.where(all_ids[None, :] == ids[:, None], block_start[None, :], 0), axis=1
        )
        return base[:, None] + (lanes[None, :] >= start[:, None]).astype(jnp.int32)

    same = records(key_ids)[:, :, None, None] == records(query_ids)[None, None, :, :]
    causal = lanes[None, :, None, None] <= lanes[None, None, None, :]
    distance = query_ids[None, :] - key_ids[:, None]
    picked = jnp.zeros(distance.shape, jnp.int32)
    for step in range(flags.shape[1]):
        picked = jnp.where(distance == step + 1, flags[None, :, step], picked)
    earlier = ((picked == 1) & (key_ids[:, None] >= 0))[:, None, :, None]
    own = (distance == 0)[:, None, :, None]
    visible = same & (earlier | (own & causal))
    bias = jnp.where(visible, 0.0, MASKED).astype(jnp.float32)
    return bias.reshape(key_ids.shape[0] * tokens, query_ids.shape[0] * tokens)


def devices_of():
    return math.prod(lax.axis_size(name) for name in ALL)


def send(value, target):
    count = devices_of()
    return lax.ppermute(value, ALL, [(source, target(source) % count) for source in range(count)])


def next_chip(value):
    return send(value, lambda source: source + 2)


def next_chip_crossed(value):
    return send(value, lambda source: (source + 2) ^ 1)


def second_next_chip(value):
    count, ring = devices_of(), lax.axis_size("y")

    def between(source):
        y = source // 2 % ring
        return source + 2 * ((y - 1) % ring - y)

    value = lax.ppermute(value, "y", [(y, (y - 1) % ring) for y in range(ring)])
    return lax.ppermute(
        value, ALL, [(between(source), (source + 4) % count) for source in range(count)]
    )


def to_sibling(value):
    return lax.ppermute(value, "c", [(0, 1), (1, 0)])


def body(q_proj, k_proj, v_proj, block_start, kv_select, pre_gate, post_gate, long_filter):
    channels, tokens = q_proj.shape
    devices = devices_of()
    group = channels // devices
    tables = make_tables(devices, tokens)
    core = lax.axis_index("c")
    first_core = core == 0

    other = pick_heads(1 - core, k_proj, v_proj)
    sibling = to_sibling(other)
    crossed = next_chip_crossed(other)
    k_later, v_later, other = lax.optimization_barrier((k_proj, v_proj, other))
    mine = pick_heads(core, k_later, v_later)
    near = next_chip(mine)
    odd = jnp.where(first_core, sibling, mine)
    far = second_next_chip(odd)
    flags = kv_select.astype(jnp.float32)
    flags = jnp.concatenate([flags, to_sibling(flags)], axis=0).astype(jnp.int32)
    first = 2 * lax.axis_index(ALL[:-1])
    key_ids = jnp.stack(
        [first - 3, first - 2 + core, first - 1 - core, first + core, first + 1 - core]
    )
    query_ids = jnp.stack([first + core, first + 1 - core])
    bias = chip_bias(block_start, flags, key_ids, query_ids, tokens)

    q_later, gate_later, bias, _ = lax.optimization_barrier((q_proj, pre_gate, bias, odd))
    exchanged_half = to_sibling(pick_heads(1 - core, q_later, gate_later))

    def exchanged(source):
        upper, zc, lower, c = source // 64, source // 32 % 2, source // 2 % 16, source % 2
        return upper * 64 + c * 32 + lower * 2 + zc

    taps = long_filter.reshape(group, devices, tokens)
    taps, bias, _ = lax.optimization_barrier((taps, bias, odd))
    taps, far, near = lax.optimization_barrier((taps, far, near))
    moved = [(source, exchanged(source)) for source in range(devices) if exchanged(source) != source]
    swapped = lax.ppermute(taps, ALL, moved)

    out_mine, out_other, gated = attend(
        core, bias, q_proj, pre_gate, exchanged_half, (far, near, crossed, mine, sibling), group
    )
    gated, swapped = lax.optimization_barrier((gated, swapped))
    taps = jnp.where(lax.axis_index("zc") == core, taps, swapped)
    spectrum = transform_filter(taps, tables)
    gathered = lax.all_to_all(gated, CHIPS, split_axis=0, concat_axis=0, tiled=True)
    out_other = to_sibling(out_other)
    attn_out = jnp.stack(
        [
            jnp.where(first_core, out_mine, out_other).reshape(STEPS, -1, tokens),
            jnp.where(first_core, out_other, out_mine).reshape(STEPS, -1, tokens),
        ],
        axis=1,
    ).reshape(channels, tokens)

    conv_out = convolve(gathered.reshape(devices, group, tokens), spectrum, tables)
    returned = lax.all_to_all(
        conv_out, OWNERS, split_axis=0, concat_axis=0, tiled=True
    ).reshape(channels, tokens)
    mixed = (post_gate.astype(jnp.float32) * returned.astype(jnp.float32)).astype(jnp.bfloat16)
    return (attn_out, mixed)


def solution(mesh):
    chips = Mesh(mesh.devices.reshape(2, 2, 2, 4, 4, 2), ALL)
    return jax.shard_map(
        body,
        mesh=chips,
        in_specs=(
            P(None, ALL),
            P(None, ALL),
            P(None, ALL),
            P(),
            P(ALL, None),
            P(None, ALL),
            P(None, ALL),
            P(ALL, None),
        ),
        out_specs=(P(None, ALL), P(None, ALL)),
        check_vma=False,
    )
```

```python
import math

import jax
import jax.numpy as jnp
import ml_dtypes
import numpy as np
from jax import lax
from jax.experimental import pallas as pl
from jax.experimental.pallas import tpu as pltpu
from jax.sharding import Mesh
from jax.sharding import PartitionSpec as P

HD = 128
ALL = ("za", "zb", "zc", "x", "y", "c")
CHIPS = ("za", "zb", "x", "y", "zc")
OWNERS = ("za", "zb", "c", "x", "y", "zc")
STEPS = 4
MASKED = -1e30
VMEM_LIMIT = 48 * 1024 * 1024
HBM_ONLY = 60 * 1024 * 1024


def hi_lo(table):
    high = table.astype(ml_dtypes.bfloat16)
    low = (table - high.astype(np.float64)).astype(ml_dtypes.bfloat16)
    return (high, low)


def make_tables(rows, width):
    length = rows * width
    k1 = np.arange(rows)[:, None]
    n1 = np.arange(rows)[None, :]
    theta = 2.0 * np.pi * (((4 * k1 + 1) * n1) % (4 * rows)) / (4 * rows)
    n2 = np.arange(width)[None, :]
    turn = 2.0 * np.pi * (((4 * k1 + 1) * n2) % (4 * length)) / (4 * length)
    k2 = np.arange(width)[:, None]
    phi = 2.0 * np.pi * ((k2 * n2) % width) / width
    first = hi_lo(np.concatenate([np.cos(theta), -np.sin(theta)], axis=0))
    second = hi_lo(np.block([[np.cos(phi), -np.sin(phi)], [np.sin(phi), np.cos(phi)]]))
    second_back = hi_lo(np.block([[np.cos(phi), np.sin(phi)], [-np.sin(phi), np.cos(phi)]]))
    first_back = hi_lo(np.concatenate([np.cos(theta).T, -np.sin(theta).T], axis=1) / length)
    twist = (np.cos(turn).astype(np.float32), -np.sin(turn).astype(np.float32))
    blocks = np.arange(rows).reshape(4, 2, -1, 2)
    arriving = blocks.transpose(0, 2, 1, 3).reshape(-1)
    leaving = blocks.transpose(0, 3, 2, 1).reshape(-1)
    first_moved = np.concatenate([table[:, arriving] for table in first], axis=1)
    first = np.concatenate(first, axis=1)
    second = np.concatenate([second[0], second[0], second[1]], axis=0)
    second_back = np.concatenate([second_back[0], second_back[0], second_back[1]], axis=0)
    high, low = (table[leaving] for table in first_back)
    first_back = np.concatenate([high, high, low], axis=1)
    return first, first_moved, twist, second, second_back, first_back


def dot(left, right):
    return jnp.dot(left, right, preferred_element_type=jnp.float32)


def split(value):
    high = value.astype(jnp.bfloat16)
    low = (value - high.astype(jnp.float32)).astype(jnp.bfloat16)
    return high, low


def turned_by(real, imag, cosine, sine):
    return real * cosine - imag * sine, real * sine + imag * cosine


def interleaved(tasks, lag=1):
    waiting, active, turn = list(tasks), [], 0
    while waiting or active:
        if waiting and turn % lag == 0:
            active.append(waiting.pop(0))
        active = [task for task in active if next(task, None) is not None]
        turn += 1


def forward(signals, first, cosine, sine, second):
    rows, width = signals[0].shape
    signal = jnp.concatenate(signals, axis=1)
    part = dot(first, jnp.concatenate([signal, signal], axis=0))
    yield part
    turned = []
    for channel in range(2):
        lanes = slice(channel * width, (channel + 1) * width)
        turned.append(
            jnp.concatenate(turned_by(part[:rows, lanes], part[rows:, lanes], cosine, sine), axis=1)
        )
    high, low = split(jnp.concatenate(turned, axis=0))
    yield dot(jnp.concatenate([high, low, high], axis=1), second)


def filter_task(pair, filter_ref, first, cosine, sine, second, out_ref):
    signals = [filter_ref[2 * pair], filter_ref[2 * pair + 1]]
    rows = signals[0].shape[0]
    for spectrum in forward(signals, first[...], cosine[...], sine[...], second[...]):
        yield True
    out_ref[2 * rows * pair : 2 * rows * (pair + 1)] = spectrum


def filter_kernel(filter_ref, *rest):
    pairs = filter_ref.shape[0] // 2
    interleaved([filter_task(pair, filter_ref, *rest) for pair in range(pairs)])


def conv_task(
    channel, place, rows, load, store, spectrum_ref, first, cosine_ref, sine_ref, second, second_back, first_back
):
    width = cosine_ref.shape[1]
    cosine, sine = cosine_ref[...], sine_ref[...]
    signals = [load(channel), load(channel + 1)]
    for spectrum in forward(signals, first[...], cosine, sine, second[...]):
        yield True
    other = spectrum_ref[rows * place : rows * (place + 2)]
    product = jnp.concatenate(
        turned_by(spectrum[:, :width], spectrum[:, width:], other[:, :width], other[:, width:]),
        axis=1,
    )
    high, low = split(product)
    part = dot(jnp.concatenate([high, low, high], axis=1), second_back[...])
    yield True
    reals, imags = [], []
    for half in range(2):
        block = part[half * rows : (half + 1) * rows]
        real, imag = turned_by(block[:, :width], block[:, width:], cosine, -sine)
        reals.append(real)
        imags.append(imag)
    turned = jnp.concatenate(
        [jnp.concatenate(reals, axis=1), jnp.concatenate(imags, axis=1)], axis=0
    )
    high, low = split(turned)
    result = dot(first_back[...], jnp.concatenate([high, low, high], axis=0))
    yield True
    store(channel, result[:, :width])
    store(channel + 1, result[:, width:])


def conv_kernel(signal_ref, spectrum_ref, *rest):
    *tables, out_ref, taken, given = rest
    rows, channels, width = signal_ref.shape
    here = spectrum_ref.shape[0] // rows
    step = pl.program_id(0)
    base = step * here

    @pl.when(step == 0)
    def _():
        taken[...] = signal_ref[...].astype(jnp.float32).reshape(taken.shape)

    def load(channel):
        return taken[pl.ds(base + channel, rows, stride=channels), :].astype(jnp.bfloat16)

    def store(channel, value):
        given[pl.ds(base + channel, rows, stride=channels), :] = value

    interleaved(
        [
            conv_task(channel, channel, rows, load, store, spectrum_ref, *tables)
            for channel in range(0, here, 2)
        ]
    )

    @pl.when(step == pl.num_programs(0) - 1)
    def _():
        out_ref[...] = given[...].reshape(out_ref.shape).astype(jnp.bfloat16)


def whole(array):
    return pl.BlockSpec(array.shape, lambda step: (0,) * array.ndim)


def transform_filter(taps, tables, step_channels=4):
    first, _, twist, second, _, _ = tables
    channels, rows, width = taps.shape
    constants = [jnp.asarray(entry) for entry in (first, *twist, second)]
    return pl.pallas_call(
        filter_kernel,
        grid=(channels // step_channels,),
        in_specs=[pl.BlockSpec((step_channels, rows, width), lambda step: (step, 0, 0))]
        + [whole(entry) for entry in constants],
        out_specs=pl.BlockSpec((step_channels * rows, 2 * width), lambda step: (step, 0)),
        out_shape=jax.ShapeDtypeStruct((channels * rows, 2 * width), jnp.float32),
        compiler_params=pltpu.CompilerParams(vmem_limit_bytes=HBM_ONLY),
        cost_estimate=pl.CostEstimate(
            flops=channels * 170_000_000, bytes_accessed=6 * 1024 * 1024, transcendentals=0
        ),
        name="filter_spectrum",
    )(taps, *constants)


def convolve(signal, spectrum, tables, step_channels=8):
    _, first, twist, second, second_back, first_back = tables
    rows, channels, width = signal.shape
    constants = [jnp.asarray(entry) for entry in (first, *twist, second, second_back, first_back)]
    return pl.pallas_call(
        conv_kernel,
        grid=(channels // step_channels,),
        in_specs=[
            whole(signal),
            pl.BlockSpec((step_channels * rows, 2 * width), lambda step: (step, 0)),
        ]
        + [whole(entry) for entry in constants],
        out_specs=whole(signal),
        out_shape=jax.ShapeDtypeStruct(signal.shape, jnp.bfloat16),
        scratch_shapes=[pltpu.VMEM((rows * channels, width), jnp.float32)] * 2,
        compiler_params=pltpu.CompilerParams(vmem_limit_bytes=HBM_ONLY),
        cost_estimate=pl.CostEstimate(
            flops=channels * 370_000_000, bytes_accessed=8 * 1024 * 1024, transcendentals=0
        ),
        name="convolve",
    )(signal, spectrum, *constants)


def pick_heads(which, first, second):
    tokens = first.shape[1]
    pairs = [value.reshape(STEPS, 2, -1, tokens) for value in (first, second)]
    return jnp.stack(
        [
            lax.dynamic_index_in_dim(pair, which, 1, keepdims=False).reshape(-1, tokens)
            for pair in pairs
        ]
    )


def attend_kernel(
    core_ref,
    bias_ref,
    q_mine,
    gate_mine,
    q_other,
    gate_other,
    far,
    near,
    crossed,
    own,
    sibling,
    out_mine,
    out_other,
    gated,
):
    heads, tokens = gate_other.shape[0] // HD, gate_other.shape[1]
    group = gated.shape[2]
    core = core_ref[0]
    pairs = (far, near, crossed, own, sibling)
    part_heads = q_mine.shape[1] // HD

    def rows_of(head):
        return slice(head * HD, (head + 1) * HD)

    def own_rows(ref, head):
        return ref[head // part_heads, rows_of(head % part_heads)]

    def task(head):
        rows = rows_of(head)
        queries = jnp.concatenate([own_rows(q_mine, head), q_other[rows]], axis=1)
        keys = jnp.concatenate([pair[0, rows] for pair in pairs], axis=1)
        scores = lax.dot_general(
            keys, queries, (((0,), (0,)), ((), ())), preferred_element_type=jnp.float32
        )
        yield True
        masked = scores * (math.log2(math.e) / math.sqrt(HD)) + bias_ref[...]
        weights = jnp.exp2(masked - jnp.max(masked, axis=0, keepdims=True))
        total = jnp.sum(weights, axis=0, keepdims=True)
        weights = weights.astype(jnp.bfloat16)
        yield True
        values = jnp.concatenate([pair[1, rows] for pair in pairs], axis=1)
        mixed = (dot(values, weights) * (1.0 / total)).astype(jnp.bfloat16)
        gates = (
            (out_mine, own_rows(gate_mine, head), core),
            (out_other, gate_other[rows], 1 - core),
        )
        for place, (out, gate, block) in enumerate(gates):
            part = mixed[:, place * tokens : (place + 1) * tokens]
            out[rows] = part
            product = (part.astype(jnp.float32) * gate.astype(jnp.float32)).astype(jnp.bfloat16)
            owners = slice(head * HD // group, (head + 1) * HD // group)
            gated[owners, block] = product.reshape(HD // group, group, tokens)

    interleaved([task(head) for head in range(heads)])


def attend(core, bias, q_proj, gate, exchanged, blocks, group, steps=2):
    channels, tokens = q_proj.shape[0] // 2, q_proj.shape[1]
    step_rows = channels // steps
    halves = [value.reshape(STEPS, 2, channels // STEPS, tokens) for value in (q_proj, gate)]
    half = pl.BlockSpec(
        (STEPS // steps, None, channels // STEPS, tokens), lambda step, core: (step, core[0], 0, 0)
    )
    single = pl.BlockSpec((step_rows, tokens), lambda step, core: (step, 0))
    pair = pl.BlockSpec((2, step_rows, tokens), lambda step, core: (0, step, 0))
    pieces = [
        pl.BlockSpec((None, step_rows, tokens), lambda step, core, which=which: (which, step, 0))
        for which in range(2)
    ]
    return pl.pallas_call(
        attend_kernel,
        grid_spec=pltpu.PrefetchScalarGridSpec(
            num_scalar_prefetch=1,
            grid=(steps,),
            in_specs=[pl.BlockSpec(bias.shape, lambda step, core: (0, 0)), half, half, *pieces]
            + [pair] * 5,
            out_specs=[
                single,
                single,
                pl.BlockSpec((step_rows // group, 2, group, tokens), lambda step, core: (step, 0, 0, 0)),
            ],
        ),
        out_shape=[
            jax.ShapeDtypeStruct((channels, tokens), jnp.bfloat16),
            jax.ShapeDtypeStruct((channels, tokens), jnp.bfloat16),
            jax.ShapeDtypeStruct((channels // group, 2, group, tokens), jnp.bfloat16),
        ],
        compiler_params=pltpu.CompilerParams(vmem_limit_bytes=HBM_ONLY),
        cost_estimate=pl.CostEstimate(
            flops=(channels // HD) * 4 * HD * bias.size,
            bytes_accessed=18 * 2 * channels * tokens + 4 * bias.size,
            transcendentals=(channels // HD) * bias.size,
        ),
        name="attend",
    )(core.reshape(1), bias, *halves, exchanged, exchanged, *blocks)


def chip_bias(block_start, flags, key_ids, query_ids, tokens):
    opened = (block_start < tokens).astype(jnp.int32)
    all_ids = jnp.arange(block_start.shape[0], dtype=jnp.int32)
    lanes = jnp.arange(tokens, dtype=jnp.int32)

    def records(ids):
        base = jnp.sum(jnp.where(all_ids[None, :] < ids[:, None], opened[None, :], 0), axis=1)
        start = jnp.sum(
            jnp.where(all_ids[None, :] == ids[:, None], block_start[None, :], 0), axis=1
        )
        return base[:, None] + (lanes[None, :] >= start[:, None]).astype(jnp.int32)

    same = records(key_ids)[:, :, None, None] == records(query_ids)[None, None, :, :]
    causal = lanes[None, :, None, None] <= lanes[None, None, None, :]
    distance = query_ids[None, :] - key_ids[:, None]
    picked = jnp.zeros(distance.shape, jnp.int32)
    for step in range(flags.shape[1]):
        picked = jnp.where(distance == step + 1, flags[None, :, step], picked)
    earlier = ((picked == 1) & (key_ids[:, None] >= 0))[:, None, :, None]
    own = (distance == 0)[:, None, :, None]
    visible = same & (earlier | (own & causal))
    bias = jnp.where(visible, 0.0, MASKED).astype(jnp.float32)
    return bias.reshape(key_ids.shape[0] * tokens, query_ids.shape[0] * tokens)


def devices_of():
    return math.prod(lax.axis_size(name) for name in ALL)


def send(value, target):
    count = devices_of()
    return lax.ppermute(value, ALL, [(source, target(source) % count) for source in range(count)])


def next_chip(value):
    return send(value, lambda source: source + 2)


def next_chip_crossed(value):
    return send(value, lambda source: (source + 2) ^ 1)


def second_next_chip(value):
    count, ring = devices_of(), lax.axis_size("y")

    def between(source):
        y = source // 2 % ring
        return source + 2 * ((y - 1) % ring - y)

    value = lax.ppermute(value, "y", [(y, (y - 1) % ring) for y in range(ring)])
    return lax.ppermute(
        value, ALL, [(between(source), (source + 4) % count) for source in range(count)]
    )


def to_sibling(value):
    return lax.ppermute(value, "c", [(0, 1), (1, 0)])


def body(q_proj, k_proj, v_proj, block_start, kv_select, pre_gate, post_gate, long_filter):
    channels, tokens = q_proj.shape
    devices = devices_of()
    group = channels // devices
    tables = make_tables(devices, tokens)
    core = lax.axis_index("c")
    first_core = core == 0

    other = pick_heads(1 - core, k_proj, v_proj)
    sibling = to_sibling(other)
    crossed = next_chip_crossed(other)
    k_later, v_later, other = lax.optimization_barrier((k_proj, v_proj, other))
    mine = pick_heads(core, k_later, v_later)
    near = next_chip(mine)
    odd = jnp.where(first_core, sibling, mine)
    far = second_next_chip(odd)
    flags = kv_select.astype(jnp.float32)
    flags = jnp.concatenate([flags, to_sibling(flags)], axis=0).astype(jnp.int32)
    first = 2 * lax.axis_index(ALL[:-1])
    key_ids = jnp.stack(
        [first - 3, first - 2 + core, first - 1 - core, first + core, first + 1 - core]
    )
    query_ids = jnp.stack([first + core, first + 1 - core])
    bias = chip_bias(block_start, flags, key_ids, query_ids, tokens)

    q_later, gate_later, bias, _ = lax.optimization_barrier((q_proj, pre_gate, bias, odd))
    exchanged_half = to_sibling(pick_heads(1 - core, q_later, gate_later))

    def exchanged(source):
        upper, zc, lower, c = source // 64, source // 32 % 2, source // 2 % 16, source % 2
        return upper * 64 + c * 32 + lower * 2 + zc

    taps = long_filter.reshape(group, devices, tokens)
    taps, bias, _ = lax.optimization_barrier((taps, bias, odd))
    taps, near, crossed = lax.optimization_barrier((taps, near, crossed))
    moved = [(source, exchanged(source)) for source in range(devices) if exchanged(source) != source]
    swapped = lax.ppermute(taps, ALL, moved)

    out_mine, out_other, gated = attend(
        core, bias, q_proj, pre_gate, exchanged_half, (far, near, crossed, mine, sibling), group
    )
    gated, swapped = lax.optimization_barrier((gated, swapped))
    taps = jnp.where(lax.axis_index("zc") == core, taps, swapped)
    spectrum = transform_filter(taps, tables)
    gathered = lax.all_to_all(gated, CHIPS, split_axis=0, concat_axis=0, tiled=True)
    out_other = to_sibling(out_other)
    attn_out = jnp.stack(
        [
            jnp.where(first_core, out_mine, out_other).reshape(STEPS, -1, tokens),
            jnp.where(first_core, out_other, out_mine).reshape(STEPS, -1, tokens),
        ],
        axis=1,
    ).reshape(channels, tokens)

    conv_out = convolve(gathered.reshape(devices, group, tokens), spectrum, tables)
    returned = lax.all_to_all(
        conv_out, OWNERS, split_axis=0, concat_axis=0, tiled=True
    ).reshape(channels, tokens)
    mixed = (post_gate.astype(jnp.float32) * returned.astype(jnp.float32)).astype(jnp.bfloat16)
    return (attn_out, mixed)


def solution(mesh):
    chips = Mesh(mesh.devices.reshape(2, 2, 2, 4, 4, 2), ALL)
    return jax.shard_map(
        body,
        mesh=chips,
        in_specs=(
            P(None, ALL),
            P(None, ALL),
            P(None, ALL),
            P(),
            P(ALL, None),
            P(None, ALL),
            P(None, ALL),
            P(ALL, None),
        ),
        out_specs=(P(None, ALL), P(None, ALL)),
        check_vma=False,
    )
```

```python
import functools
import math

import jax
import jax.numpy as jnp
import ml_dtypes
import numpy as np
from jax import lax
from jax.experimental import pallas as pl
from jax.experimental.pallas import tpu as pltpu
from jax.sharding import Mesh
from jax.sharding import PartitionSpec as P

HD = 128
ALL = ("za", "zb", "zc", "x", "y", "c")
CHIPS = ("za", "zb", "x", "y", "zc")
OWNERS = ("za", "zb", "c", "x", "y", "zc")
STEPS = 4
MASKED = -1e30
VMEM_LIMIT = 48 * 1024 * 1024
HBM_ONLY = 60 * 1024 * 1024


def hi_lo(table):
    high = table.astype(ml_dtypes.bfloat16)
    low = (table - high.astype(np.float64)).astype(ml_dtypes.bfloat16)
    return (high, low)


def make_tables(rows, width):
    length = rows * width
    k1 = np.arange(rows)[:, None]
    n1 = np.arange(rows)[None, :]
    theta = 2.0 * np.pi * (((4 * k1 + 1) * n1) % (4 * rows)) / (4 * rows)
    n2 = np.arange(width)[None, :]
    turn = 2.0 * np.pi * (((4 * k1 + 1) * n2) % (4 * length)) / (4 * length)
    k2 = np.arange(width)[:, None]
    phi = 2.0 * np.pi * ((k2 * n2) % width) / width
    first = hi_lo(np.concatenate([np.cos(theta), -np.sin(theta)], axis=0))
    second = hi_lo(np.block([[np.cos(phi), -np.sin(phi)], [np.sin(phi), np.cos(phi)]]))
    second_back = hi_lo(np.block([[np.cos(phi), np.sin(phi)], [-np.sin(phi), np.cos(phi)]]))
    first_back = hi_lo(np.concatenate([np.cos(theta).T, -np.sin(theta).T], axis=1) / length)
    twist = (np.cos(turn).astype(np.float32), -np.sin(turn).astype(np.float32))
    blocks = np.arange(rows).reshape(4, 2, -1, 2)
    arriving = blocks.transpose(0, 2, 1, 3).reshape(-1)
    leaving = blocks.transpose(0, 3, 2, 1).reshape(-1)
    first_moved = np.concatenate([table[:, arriving] for table in first], axis=1)
    first = np.concatenate(first, axis=1)
    second = np.concatenate([second[0], second[0], second[1]], axis=0)
    second_back = np.concatenate([second_back[0], second_back[0], second_back[1]], axis=0)
    high, low = (table[leaving] for table in first_back)
    first_back = np.concatenate([high, high, low], axis=1)
    return first, first_moved, twist, second, second_back, first_back


def dot(left, right):
    return jnp.dot(left, right, preferred_element_type=jnp.float32)


def split(value):
    high = value.astype(jnp.bfloat16)
    low = (value - high.astype(jnp.float32)).astype(jnp.bfloat16)
    return high, low


def turned_by(real, imag, cosine, sine):
    return real * cosine - imag * sine, real * sine + imag * cosine


def interleaved(tasks, lag=1):
    waiting, active, turn = list(tasks), [], 0
    while waiting or active:
        if waiting and turn % lag == 0:
            active.append(waiting.pop(0))
        active = [task for task in active if next(task, None) is not None]
        turn += 1


def forward(signals, first, cosine, sine, second):
    rows, width = signals[0].shape
    signal = jnp.concatenate(signals, axis=1)
    part = dot(first, jnp.concatenate([signal, signal], axis=0))
    yield part
    turned = []
    for channel in range(2):
        lanes = slice(channel * width, (channel + 1) * width)
        turned.append(
            jnp.concatenate(turned_by(part[:rows, lanes], part[rows:, lanes], cosine, sine), axis=1)
        )
    high, low = split(jnp.concatenate(turned, axis=0))
    yield dot(jnp.concatenate([high, low, high], axis=1), second)


def filter_task(pair, filter_ref, first, cosine, sine, second, out_ref):
    signals = [filter_ref[2 * pair], filter_ref[2 * pair + 1]]
    rows = signals[0].shape[0]
    for spectrum in forward(signals, first[...], cosine[...], sine[...], second[...]):
        yield True
    out_ref[2 * rows * pair : 2 * rows * (pair + 1)] = spectrum


def filter_kernel(filter_ref, *rest):
    pairs = filter_ref.shape[0] // 2
    interleaved([filter_task(pair, filter_ref, *rest) for pair in range(pairs)])


def conv_task(
    channel, place, rows, load, store, spectrum_ref, first, cosine_ref, sine_ref, second, second_back, first_back
):
    width = cosine_ref.shape[1]
    cosine, sine = cosine_ref[...], sine_ref[...]
    signals = [load(channel), load(channel + 1)]
    for spectrum in forward(signals, first[...], cosine, sine, second[...]):
        yield True
    other = spectrum_ref[rows * place : rows * (place + 2)]
    product = jnp.concatenate(
        turned_by(spectrum[:, :width], spectrum[:, width:], other[:, :width], other[:, width:]),
        axis=1,
    )
    high, low = split(product)
    part = dot(jnp.concatenate([high, low, high], axis=1), second_back[...])
    yield True
    reals, imags = [], []
    for half in range(2):
        block = part[half * rows : (half + 1) * rows]
        real, imag = turned_by(block[:, :width], block[:, width:], cosine, -sine)
        reals.append(real)
        imags.append(imag)
    turned = jnp.concatenate(
        [jnp.concatenate(reals, axis=1), jnp.concatenate(imags, axis=1)], axis=0
    )
    high, low = split(turned)
    result = dot(first_back[...], jnp.concatenate([high, low, high], axis=0))
    yield True
    store(channel, result[:, :width])
    store(channel + 1, result[:, width:])


def conv_kernel(signal_ref, spectrum_ref, *rest):
    *tables, out_ref, taken, given = rest
    rows, channels, width = signal_ref.shape
    here = spectrum_ref.shape[0] // rows
    step = pl.program_id(0)
    base = step * here

    @pl.when(step == 0)
    def _():
        taken[...] = signal_ref[...].astype(jnp.float32).reshape(taken.shape)

    def load(channel):
        return taken[pl.ds(base + channel, rows, stride=channels), :].astype(jnp.bfloat16)

    def store(channel, value):
        given[pl.ds(base + channel, rows, stride=channels), :] = value

    interleaved(
        [
            conv_task(channel, channel, rows, load, store, spectrum_ref, *tables)
            for channel in range(0, here, 2)
        ]
    )

    @pl.when(step == pl.num_programs(0) - 1)
    def _():
        out_ref[...] = given[...].reshape(out_ref.shape).astype(jnp.bfloat16)


def whole(array):
    return pl.BlockSpec(array.shape, lambda step: (0,) * array.ndim)


def transform_filter(taps, tables, step_channels=4):
    first, _, twist, second, _, _ = tables
    channels, rows, width = taps.shape
    constants = [jnp.asarray(entry) for entry in (first, *twist, second)]
    return pl.pallas_call(
        filter_kernel,
        grid=(channels // step_channels,),
        in_specs=[pl.BlockSpec((step_channels, rows, width), lambda step: (step, 0, 0))]
        + [whole(entry) for entry in constants],
        out_specs=pl.BlockSpec((step_channels * rows, 2 * width), lambda step: (step, 0)),
        out_shape=jax.ShapeDtypeStruct((channels * rows, 2 * width), jnp.float32),
        compiler_params=pltpu.CompilerParams(vmem_limit_bytes=HBM_ONLY),
        cost_estimate=pl.CostEstimate(
            flops=channels * 170_000_000, bytes_accessed=6 * 1024 * 1024, transcendentals=0
        ),
        name="filter_spectrum",
    )(taps, *constants)


def convolve(signal, spectrum, tables, step_channels=8):
    _, first, twist, second, second_back, first_back = tables
    rows, channels, width = signal.shape
    constants = [jnp.asarray(entry) for entry in (first, *twist, second, second_back, first_back)]
    return pl.pallas_call(
        conv_kernel,
        grid=(channels // step_channels,),
        in_specs=[
            whole(signal),
            pl.BlockSpec((step_channels * rows, 2 * width), lambda step: (step, 0)),
        ]
        + [whole(entry) for entry in constants],
        out_specs=whole(signal),
        out_shape=jax.ShapeDtypeStruct(signal.shape, jnp.bfloat16),
        scratch_shapes=[pltpu.VMEM((rows * channels, width), jnp.float32)] * 2,
        compiler_params=pltpu.CompilerParams(vmem_limit_bytes=HBM_ONLY),
        cost_estimate=pl.CostEstimate(
            flops=channels * 370_000_000, bytes_accessed=8 * 1024 * 1024, transcendentals=0
        ),
        name="convolve",
    )(signal, spectrum, *constants)


def pick_heads(which, first, second):
    tokens = first.shape[1]
    pairs = [value.reshape(STEPS, 2, -1, tokens) for value in (first, second)]
    return jnp.stack(
        [
            lax.dynamic_index_in_dim(pair, which, 1, keepdims=False).reshape(-1, tokens)
            for pair in pairs
        ]
    )


def attend_kernel(
    parity, core_ref, bias_ref, q_mine, gate_mine, q_other, gate_other, near, crossed, own, sibling, *rest
):
    out_ref, gated = rest[-2:]
    heads, tokens = gate_other.shape[0] // HD, gate_other.shape[1]
    group = gated.shape[1]
    is_mine = core_ref[0] == parity
    part_heads = q_mine.shape[1] // HD

    def rows_of(head):
        return slice(head * HD, (head + 1) * HD)

    def chosen(mine_ref, other_ref, head):
        mine = mine_ref[head // part_heads, rows_of(head % part_heads)]
        return jnp.where(is_mine, mine, other_ref[rows_of(head)])

    def window(kind, rows):
        shared = [near[kind, rows], crossed[kind, rows]]
        if parity == 1:
            return jnp.concatenate(shared + [own[kind, rows], sibling[kind, rows]], axis=1)
        itself = jnp.where(is_mine, own[kind, rows], sibling[kind, rows])
        return jnp.concatenate(shared + [rest[0][kind, rows], itself], axis=1)

    def task(head):
        rows = rows_of(head)
        scores = lax.dot_general(
            window(0, rows),
            chosen(q_mine, q_other, head),
            (((0,), (0,)), ((), ())),
            preferred_element_type=jnp.float32,
        )
        yield True
        masked = scores * (math.log2(math.e) / math.sqrt(HD)) + bias_ref[...]
        weights = jnp.exp2(masked - jnp.max(masked, axis=0, keepdims=True))
        total = jnp.sum(weights, axis=0, keepdims=True)
        weights = weights.astype(jnp.bfloat16)
        yield True
        mixed = (dot(window(1, rows), weights) * (1.0 / total)).astype(jnp.bfloat16)
        out_ref[rows] = mixed
        gate = chosen(gate_mine, gate_other, head)
        product = (mixed.astype(jnp.float32) * gate.astype(jnp.float32)).astype(jnp.bfloat16)
        owners = slice(head * HD // group, (head + 1) * HD // group)
        gated[owners] = product.reshape(HD // group, group, tokens)

    interleaved([task(head) for head in range(heads)])


def attend(parity, core, bias, q_proj, gate, exchanged, blocks, group, gated=None, steps=2):
    channels, tokens = q_proj.shape[0] // 2, q_proj.shape[1]
    step_rows = channels // steps
    halves = [value.reshape(STEPS, 2, channels // STEPS, tokens) for value in (q_proj, gate)]
    half = pl.BlockSpec(
        (STEPS // steps, None, channels // STEPS, tokens), lambda step, core: (step, core[0], 0, 0)
    )
    pair = pl.BlockSpec((2, step_rows, tokens), lambda step, core: (0, step, 0))
    pieces = [
        pl.BlockSpec((None, step_rows, tokens), lambda step, core, which=which: (which, step, 0))
        for which in range(2)
    ]
    operands = [core.reshape(1), bias, *halves, exchanged, exchanged, *blocks]
    in_specs = [pl.BlockSpec(bias.shape, lambda step, core: (0, 0)), half, half, *pieces]
    in_specs += [pair] * len(blocks)
    aliases = {}
    if gated is not None:
        aliases = {len(operands): 1}
        operands.append(gated)
        in_specs.append(pl.BlockSpec(memory_space=pl.ANY))
    return pl.pallas_call(
        functools.partial(attend_kernel, parity),
        grid_spec=pltpu.PrefetchScalarGridSpec(
            num_scalar_prefetch=1,
            grid=(steps,),
            in_specs=in_specs,
            out_specs=[
                pl.BlockSpec((step_rows, tokens), lambda step, core: (step, 0)),
                pl.BlockSpec(
                    (step_rows // group, None, group, tokens), lambda step, core: (step, parity, 0, 0)
                ),
            ],
        ),
        out_shape=[
            jax.ShapeDtypeStruct((channels, tokens), jnp.bfloat16),
            jax.ShapeDtypeStruct((channels // group, 2, group, tokens), jnp.bfloat16),
        ],
        input_output_aliases=aliases,
        compiler_params=pltpu.CompilerParams(vmem_limit_bytes=HBM_ONLY),
        cost_estimate=pl.CostEstimate(
            flops=(channels // HD) * 4 * HD * bias.size,
            bytes_accessed=16 * 2 * channels * tokens + 4 * bias.size,
            transcendentals=(channels // HD) * bias.size,
        ),
        name=("attend_first", "attend_second")[parity],
    )(*operands)


def chip_bias(block_start, flags, key_ids, query_ids, tokens):
    opened = (block_start < tokens).astype(jnp.int32)
    all_ids = jnp.arange(block_start.shape[0], dtype=jnp.int32)
    lanes = jnp.arange(tokens, dtype=jnp.int32)

    def records(ids):
        base = jnp.sum(jnp.where(all_ids[None, :] < ids[:, None], opened[None, :], 0), axis=1)
        start = jnp.sum(
            jnp.where(all_ids[None, :] == ids[:, None], block_start[None, :], 0), axis=1
        )
        return base[:, None] + (lanes[None, :] >= start[:, None]).astype(jnp.int32)

    same = records(key_ids)[:, :, None, None] == records(query_ids)[None, None, :, :]
    causal = lanes[None, :, None, None] <= lanes[None, None, None, :]
    distance = query_ids[None, :] - key_ids[:, None]
    picked = jnp.zeros(distance.shape, jnp.int32)
    for step in range(flags.shape[1]):
        picked = jnp.where(distance == step + 1, flags[None, :, step], picked)
    earlier = ((picked == 1) & (key_ids[:, None] >= 0))[:, None, :, None]
    own = (distance == 0)[:, None, :, None]
    visible = same & (earlier | (own & causal))
    bias = jnp.where(visible, 0.0, MASKED).astype(jnp.float32)
    return bias.reshape(key_ids.shape[0] * tokens, query_ids.shape[0] * tokens)


def devices_of():
    return math.prod(lax.axis_size(name) for name in ALL)


def send(value, target):
    count = devices_of()
    return lax.ppermute(value, ALL, [(source, target(source) % count) for source in range(count)])


def next_chip(value):
    return send(value, lambda source: source + 2)


def next_chip_crossed(value):
    return send(value, lambda source: (source + 2) ^ 1)


def second_next_chip(value):
    count, ring = devices_of(), lax.axis_size("y")

    def between(source):
        y = source // 2 % ring
        return source + 2 * ((y - 1) % ring - y)

    value = lax.ppermute(value, "y", [(y, (y - 1) % ring) for y in range(ring)])
    return lax.ppermute(
        value, ALL, [(between(source), (source + 4) % count) for source in range(count)]
    )


def to_sibling(value):
    return lax.ppermute(value, "c", [(0, 1), (1, 0)])


def body(q_proj, k_proj, v_proj, block_start, kv_select, pre_gate, post_gate, long_filter):
    channels, tokens = q_proj.shape
    devices = devices_of()
    group = channels // devices
    tables = make_tables(devices, tokens)
    core = lax.axis_index("c")
    first_core = core == 0

    other = pick_heads(1 - core, k_proj, v_proj)
    sibling = to_sibling(other)
    crossed = next_chip_crossed(other)
    k_later, v_later, other = lax.optimization_barrier((k_proj, v_proj, other))
    mine = pick_heads(core, k_later, v_later)
    near = next_chip(mine)
    odd = jnp.where(first_core, sibling, mine)
    far = second_next_chip(odd)
    flags = kv_select.astype(jnp.float32)
    flags = jnp.concatenate([flags, to_sibling(flags)], axis=0).astype(jnp.int32)
    first = 2 * lax.axis_index(ALL[:-1])
    near_ids = [first - 2 + core, first - 1 - core]
    windows = [[first - 3, first], [first + core, first + 1 - core]]
    biases = [
        chip_bias(
            block_start,
            jnp.where(core == parity, flags[:1], flags[1:]),
            jnp.stack(near_ids + windows[parity]),
            jnp.stack([first + parity]),
            tokens,
        )
        for parity in range(2)
    ]

    q_later, gate_later, biases, _ = lax.optimization_barrier((q_proj, pre_gate, biases, odd))
    exchanged_half = to_sibling(pick_heads(1 - core, q_later, gate_later))

    def exchanged(source):
        upper, zc, lower, c = source // 64, source // 32 % 2, source // 2 % 16, source % 2
        return upper * 64 + c * 32 + lower * 2 + zc

    taps = long_filter.reshape(group, devices, tokens)
    taps, biases, _ = lax.optimization_barrier((taps, biases, odd))
    taps, near, crossed = lax.optimization_barrier((taps, near, crossed))
    moved = [(source, exchanged(source)) for source in range(devices) if exchanged(source) != source]
    swapped = lax.ppermute(taps, ALL, moved)

    near_blocks = (near, crossed, mine, sibling)
    out_second, gated = attend(1, core, biases[1], q_proj, pre_gate, exchanged_half, near_blocks, group)
    out_first, gated = attend(
        0, core, biases[0], q_proj, pre_gate, exchanged_half, (*near_blocks, far), group, gated
    )
    gated, swapped = lax.optimization_barrier((gated, swapped))
    taps = jnp.where(lax.axis_index("zc") == core, taps, swapped)
    spectrum = transform_filter(taps, tables)
    gathered = lax.all_to_all(gated, CHIPS, split_axis=0, concat_axis=0, tiled=True)
    out_mine = jnp.where(first_core, out_first, out_second)
    out_other = to_sibling(jnp.where(first_core, out_second, out_first))
    attn_out = jnp.stack(
        [
            jnp.where(first_core, out_mine, out_other).reshape(STEPS, -1, tokens),
            jnp.where(first_core, out_other, out_mine).reshape(STEPS, -1, tokens),
        ],
        axis=1,
    ).reshape(channels, tokens)

    conv_out = convolve(gathered.reshape(devices, group, tokens), spectrum, tables)
    returned = lax.all_to_all(
        conv_out, OWNERS, split_axis=0, concat_axis=0, tiled=True
    ).reshape(channels, tokens)
    mixed = (post_gate.astype(jnp.float32) * returned.astype(jnp.float32)).astype(jnp.bfloat16)
    return (attn_out, mixed)


def solution(mesh):
    chips = Mesh(mesh.devices.reshape(2, 2, 2, 4, 4, 2), ALL)
    return jax.shard_map(
        body,
        mesh=chips,
        in_specs=(
            P(None, ALL),
            P(None, ALL),
            P(None, ALL),
            P(),
            P(ALL, None),
            P(None, ALL),
            P(None, ALL),
            P(ALL, None),
        ),
        out_specs=(P(None, ALL), P(None, ALL)),
        check_vma=False,
    )
```

```python
import functools
import math

import jax
import jax.numpy as jnp
import ml_dtypes
import numpy as np
from jax import lax
from jax.experimental import pallas as pl
from jax.experimental.pallas import tpu as pltpu
from jax.sharding import Mesh
from jax.sharding import PartitionSpec as P

HD = 128
ALL = ("za", "zb", "zc", "x", "y", "c")
CHIPS = ("za", "zb", "x", "y", "zc")
OWNERS = ("za", "zb", "c", "x", "y", "zc")
STEPS = 4
MASKED = -1e30
VMEM_LIMIT = 48 * 1024 * 1024
HBM_ONLY = 60 * 1024 * 1024


def hi_lo(table):
    high = table.astype(ml_dtypes.bfloat16)
    low = (table - high.astype(np.float64)).astype(ml_dtypes.bfloat16)
    return (high, low)


def make_tables(rows, width):
    length = rows * width
    k1 = np.arange(rows)[:, None]
    n1 = np.arange(rows)[None, :]
    theta = 2.0 * np.pi * (((4 * k1 + 1) * n1) % (4 * rows)) / (4 * rows)
    n2 = np.arange(width)[None, :]
    turn = 2.0 * np.pi * (((4 * k1 + 1) * n2) % (4 * length)) / (4 * length)
    k2 = np.arange(width)[:, None]
    phi = 2.0 * np.pi * ((k2 * n2) % width) / width
    first = hi_lo(np.concatenate([np.cos(theta), -np.sin(theta)], axis=0))
    second = hi_lo(np.block([[np.cos(phi), -np.sin(phi)], [np.sin(phi), np.cos(phi)]]))
    second_back = hi_lo(np.block([[np.cos(phi), np.sin(phi)], [-np.sin(phi), np.cos(phi)]]))
    first_back = hi_lo(np.concatenate([np.cos(theta).T, -np.sin(theta).T], axis=1) / length)
    twist = (np.cos(turn).astype(np.float32), -np.sin(turn).astype(np.float32))
    blocks = np.arange(rows).reshape(4, 2, -1, 2)
    arriving = blocks.transpose(0, 2, 1, 3).reshape(-1)
    leaving = blocks.transpose(0, 3, 2, 1).reshape(-1)
    first_moved = np.concatenate([table[:, arriving] for table in first], axis=1)
    first = np.concatenate(first, axis=1)
    second = np.concatenate([second[0], second[0], second[1]], axis=0)
    second_back = np.concatenate([second_back[0], second_back[0], second_back[1]], axis=0)
    high, low = (table[leaving] for table in first_back)
    first_back = np.concatenate([high, high, low], axis=1)
    return first, first_moved, twist, second, second_back, first_back


def dot(left, right):
    return jnp.dot(left, right, preferred_element_type=jnp.float32)


def split(value):
    high = value.astype(jnp.bfloat16)
    low = (value - high.astype(jnp.float32)).astype(jnp.bfloat16)
    return high, low


def turned_by(real, imag, cosine, sine):
    return real * cosine - imag * sine, real * sine + imag * cosine


def interleaved(tasks, lag=1):
    waiting, active, turn = list(tasks), [], 0
    while waiting or active:
        if waiting and turn % lag == 0:
            active.append(waiting.pop(0))
        active = [task for task in active if next(task, None) is not None]
        turn += 1


def forward(signals, first, cosine, sine, second):
    rows, width = signals[0].shape
    signal = jnp.concatenate(signals, axis=1)
    part = dot(first, jnp.concatenate([signal, signal], axis=0))
    yield part
    turned = []
    for channel in range(2):
        lanes = slice(channel * width, (channel + 1) * width)
        turned.append(
            jnp.concatenate(turned_by(part[:rows, lanes], part[rows:, lanes], cosine, sine), axis=1)
        )
    high, low = split(jnp.concatenate(turned, axis=0))
    yield dot(jnp.concatenate([high, low, high], axis=1), second)


def filter_task(pair, filter_ref, first, cosine, sine, second, out_ref):
    signals = [filter_ref[2 * pair], filter_ref[2 * pair + 1]]
    rows = signals[0].shape[0]
    for spectrum in forward(signals, first[...], cosine[...], sine[...], second[...]):
        yield True
    out_ref[2 * rows * pair : 2 * rows * (pair + 1)] = spectrum


def filter_kernel(filter_ref, *rest):
    pairs = filter_ref.shape[0] // 2
    interleaved([filter_task(pair, filter_ref, *rest) for pair in range(pairs)])


def conv_task(
    channel, place, rows, load, store, spectrum_ref, first, cosine_ref, sine_ref, second, second_back, first_back
):
    width = cosine_ref.shape[1]
    cosine, sine = cosine_ref[...], sine_ref[...]
    signals = [load(channel), load(channel + 1)]
    for spectrum in forward(signals, first[...], cosine, sine, second[...]):
        yield True
    other = spectrum_ref[rows * place : rows * (place + 2)]
    product = jnp.concatenate(
        turned_by(spectrum[:, :width], spectrum[:, width:], other[:, :width], other[:, width:]),
        axis=1,
    )
    high, low = split(product)
    part = dot(jnp.concatenate([high, low, high], axis=1), second_back[...])
    yield True
    reals, imags = [], []
    for half in range(2):
        block = part[half * rows : (half + 1) * rows]
        real, imag = turned_by(block[:, :width], block[:, width:], cosine, -sine)
        reals.append(real)
        imags.append(imag)
    turned = jnp.concatenate(
        [jnp.concatenate(reals, axis=1), jnp.concatenate(imags, axis=1)], axis=0
    )
    high, low = split(turned)
    result = dot(first_back[...], jnp.concatenate([high, low, high], axis=0))
    yield True
    store(channel, result[:, :width])
    store(channel + 1, result[:, width:])


def conv_kernel(signal_ref, spectrum_ref, *rest):
    *tables, out_ref, taken, given = rest
    rows, channels, width = signal_ref.shape
    here = spectrum_ref.shape[0] // rows
    step = pl.program_id(0)
    base = step * here

    @pl.when(step == 0)
    def _():
        taken[...] = signal_ref[...].astype(jnp.float32).reshape(taken.shape)

    def load(channel):
        return taken[pl.ds(base + channel, rows, stride=channels), :].astype(jnp.bfloat16)

    def store(channel, value):
        given[pl.ds(base + channel, rows, stride=channels), :] = value

    interleaved(
        [
            conv_task(channel, channel, rows, load, store, spectrum_ref, *tables)
            for channel in range(0, here, 2)
        ]
    )

    @pl.when(step == pl.num_programs(0) - 1)
    def _():
        out_ref[...] = given[...].reshape(out_ref.shape).astype(jnp.bfloat16)


def whole(array):
    return pl.BlockSpec(array.shape, lambda step: (0,) * array.ndim)


def transform_filter(taps, tables, step_channels=4):
    first, _, twist, second, _, _ = tables
    channels, rows, width = taps.shape
    constants = [jnp.asarray(entry) for entry in (first, *twist, second)]
    return pl.pallas_call(
        filter_kernel,
        grid=(channels // step_channels,),
        in_specs=[pl.BlockSpec((step_channels, rows, width), lambda step: (step, 0, 0))]
        + [whole(entry) for entry in constants],
        out_specs=pl.BlockSpec((step_channels * rows, 2 * width), lambda step: (step, 0)),
        out_shape=jax.ShapeDtypeStruct((channels * rows, 2 * width), jnp.float32),
        compiler_params=pltpu.CompilerParams(vmem_limit_bytes=HBM_ONLY),
        cost_estimate=pl.CostEstimate(
            flops=channels * 170_000_000, bytes_accessed=6 * 1024 * 1024, transcendentals=0
        ),
        name="filter_spectrum",
    )(taps, *constants)


def convolve(signal, spectrum, tables, step_channels=8):
    _, first, twist, second, second_back, first_back = tables
    rows, channels, width = signal.shape
    constants = [jnp.asarray(entry) for entry in (first, *twist, second, second_back, first_back)]
    return pl.pallas_call(
        conv_kernel,
        grid=(channels // step_channels,),
        in_specs=[
            whole(signal),
            pl.BlockSpec((step_channels * rows, 2 * width), lambda step: (step, 0)),
        ]
        + [whole(entry) for entry in constants],
        out_specs=whole(signal),
        out_shape=jax.ShapeDtypeStruct(signal.shape, jnp.bfloat16),
        scratch_shapes=[pltpu.VMEM((rows * channels, width), jnp.float32)] * 2,
        compiler_params=pltpu.CompilerParams(vmem_limit_bytes=HBM_ONLY),
        cost_estimate=pl.CostEstimate(
            flops=channels * 370_000_000, bytes_accessed=8 * 1024 * 1024, transcendentals=0
        ),
        name="convolve",
    )(signal, spectrum, *constants)


def pick_heads(which, first, second):
    tokens = first.shape[1]
    pairs = [value.reshape(STEPS, 2, -1, tokens) for value in (first, second)]
    return jnp.stack(
        [
            lax.dynamic_index_in_dim(pair, which, 1, keepdims=False).reshape(-1, tokens)
            for pair in pairs
        ]
    )


def attend_kernel(
    parity, core_ref, bias_ref, q_mine, gate_mine, q_other, gate_other, near, crossed, own, sibling, *rest
):
    out_ref, gated = rest[-2:]
    heads, tokens = gate_other.shape[0] // HD, gate_other.shape[1]
    group = gated.shape[1]
    is_mine = core_ref[0] == parity
    part_heads = q_mine.shape[1] // HD

    def rows_of(head):
        return slice(head * HD, (head + 1) * HD)

    def chosen(mine_ref, other_ref, head):
        mine = mine_ref[head // part_heads, rows_of(head % part_heads)]
        return jnp.where(is_mine, mine, other_ref[rows_of(head)])

    def window(kind, rows):
        shared = [near[kind, rows], crossed[kind, rows]]
        if parity == 1:
            return jnp.concatenate(shared + [own[kind, rows], sibling[kind, rows]], axis=1)
        itself = jnp.where(is_mine, own[kind, rows], sibling[kind, rows])
        return jnp.concatenate(shared + [rest[0][kind, rows], itself], axis=1)

    def task(head):
        rows = rows_of(head)
        scores = lax.dot_general(
            window(0, rows),
            chosen(q_mine, q_other, head),
            (((0,), (0,)), ((), ())),
            preferred_element_type=jnp.float32,
        )
        yield True
        masked = scores * (math.log2(math.e) / math.sqrt(HD)) + bias_ref[...]
        weights = jnp.exp2(masked - jnp.max(masked, axis=0, keepdims=True))
        total = jnp.sum(weights, axis=0, keepdims=True)
        weights = weights.astype(jnp.bfloat16)
        yield True
        mixed = (dot(window(1, rows), weights) * (1.0 / total)).astype(jnp.bfloat16)
        out_ref[rows] = mixed
        gate = chosen(gate_mine, gate_other, head)
        product = (mixed.astype(jnp.float32) * gate.astype(jnp.float32)).astype(jnp.bfloat16)
        owners = slice(head * HD // group, (head + 1) * HD // group)
        gated[owners] = product.reshape(HD // group, group, tokens)

    interleaved([task(head) for head in range(heads)])


def attend(parity, core, bias, q_proj, gate, exchanged, blocks, group, gated=None, steps=2):
    channels, tokens = q_proj.shape[0] // 2, q_proj.shape[1]
    step_rows = channels // steps
    halves = [value.reshape(STEPS, 2, channels // STEPS, tokens) for value in (q_proj, gate)]
    half = pl.BlockSpec(
        (STEPS // steps, None, channels // STEPS, tokens), lambda step, core: (step, core[0], 0, 0)
    )
    pair = pl.BlockSpec((2, step_rows, tokens), lambda step, core: (0, step, 0))
    pieces = [
        pl.BlockSpec((None, step_rows, tokens), lambda step, core, which=which: (which, step, 0))
        for which in range(2)
    ]
    operands = [core.reshape(1), bias, *halves, exchanged, exchanged, *blocks]
    in_specs = [pl.BlockSpec(bias.shape, lambda step, core: (0, 0)), half, half, *pieces]
    in_specs += [pair] * len(blocks)
    aliases = {}
    if gated is not None:
        aliases = {len(operands): 1}
        operands.append(gated)
        in_specs.append(pl.BlockSpec(memory_space=pl.ANY))
    return pl.pallas_call(
        functools.partial(attend_kernel, parity),
        grid_spec=pltpu.PrefetchScalarGridSpec(
            num_scalar_prefetch=1,
            grid=(steps,),
            in_specs=in_specs,
            out_specs=[
                pl.BlockSpec((step_rows, tokens), lambda step, core: (step, 0)),
                pl.BlockSpec(
                    (step_rows // group, None, group, tokens), lambda step, core: (step, parity, 0, 0)
                ),
            ],
        ),
        out_shape=[
            jax.ShapeDtypeStruct((channels, tokens), jnp.bfloat16),
            jax.ShapeDtypeStruct((channels // group, 2, group, tokens), jnp.bfloat16),
        ],
        input_output_aliases=aliases,
        compiler_params=pltpu.CompilerParams(vmem_limit_bytes=HBM_ONLY),
        cost_estimate=pl.CostEstimate(
            flops=(channels // HD) * 4 * HD * bias.size,
            bytes_accessed=16 * 2 * channels * tokens + 4 * bias.size,
            transcendentals=(channels // HD) * bias.size,
        ),
        name=("attend_first", "attend_second")[parity],
    )(*operands)


def chip_bias(block_start, flags, key_ids, query_ids, tokens):
    opened = (block_start < tokens).astype(jnp.int32)
    all_ids = jnp.arange(block_start.shape[0], dtype=jnp.int32)
    lanes = jnp.arange(tokens, dtype=jnp.int32)

    def records(ids):
        base = jnp.sum(jnp.where(all_ids[None, :] < ids[:, None], opened[None, :], 0), axis=1)
        start = jnp.sum(
            jnp.where(all_ids[None, :] == ids[:, None], block_start[None, :], 0), axis=1
        )
        return base[:, None] + (lanes[None, :] >= start[:, None]).astype(jnp.int32)

    same = records(key_ids)[:, :, None, None] == records(query_ids)[None, None, :, :]
    causal = lanes[None, :, None, None] <= lanes[None, None, None, :]
    distance = query_ids[None, :] - key_ids[:, None]
    picked = jnp.zeros(distance.shape, jnp.int32)
    for step in range(flags.shape[1]):
        picked = jnp.where(distance == step + 1, flags[None, :, step], picked)
    earlier = ((picked == 1) & (key_ids[:, None] >= 0))[:, None, :, None]
    own = (distance == 0)[:, None, :, None]
    visible = same & (earlier | (own & causal))
    bias = jnp.where(visible, 0.0, MASKED).astype(jnp.float32)
    return bias.reshape(key_ids.shape[0] * tokens, query_ids.shape[0] * tokens)


def devices_of():
    return math.prod(lax.axis_size(name) for name in ALL)


def send(value, target):
    count = devices_of()
    return lax.ppermute(value, ALL, [(source, target(source) % count) for source in range(count)])


def next_chip(value):
    return send(value, lambda source: source + 2)


def next_chip_crossed(value):
    return send(value, lambda source: (source + 2) ^ 1)


def second_next_chip(value):
    count, ring = devices_of(), lax.axis_size("y")

    def between(source):
        y = source // 2 % ring
        return source + 2 * ((y - 1) % ring - y)

    value = lax.ppermute(value, "y", [(y, (y - 1) % ring) for y in range(ring)])
    return lax.ppermute(
        value, ALL, [(between(source), (source + 4) % count) for source in range(count)]
    )


def to_sibling(value):
    return lax.ppermute(value, "c", [(0, 1), (1, 0)])


def body(q_proj, k_proj, v_proj, block_start, kv_select, pre_gate, post_gate, long_filter):
    channels, tokens = q_proj.shape
    devices = devices_of()
    group = channels // devices
    tables = make_tables(devices, tokens)
    core = lax.axis_index("c")
    first_core = core == 0

    other = pick_heads(1 - core, k_proj, v_proj)
    sibling = to_sibling(other)
    crossed = next_chip_crossed(other)
    k_later, v_later, other = lax.optimization_barrier((k_proj, v_proj, other))
    mine = pick_heads(core, k_later, v_later)
    near = next_chip(mine)
    odd = jnp.where(first_core, sibling, mine)
    starts, picked, odd = lax.optimization_barrier((block_start, kv_select, odd))
    far = second_next_chip(odd)
    flags = picked.astype(jnp.float32)
    flags = jnp.concatenate([flags, to_sibling(flags)], axis=0).astype(jnp.int32)
    first = 2 * lax.axis_index(ALL[:-1])
    near_ids = [first - 2 + core, first - 1 - core]
    windows = [[first - 3, first], [first + core, first + 1 - core]]
    biases = [
        chip_bias(
            starts,
            jnp.where(core == parity, flags[:1], flags[1:]),
            jnp.stack(near_ids + windows[parity]),
            jnp.stack([first + parity]),
            tokens,
        )
        for parity in range(2)
    ]

    q_later, gate_later, biases, _ = lax.optimization_barrier((q_proj, pre_gate, biases, odd))
    exchanged_half = to_sibling(pick_heads(1 - core, q_later, gate_later))

    def exchanged(source):
        upper, zc, lower, c = source // 64, source // 32 % 2, source // 2 % 16, source % 2
        return upper * 64 + c * 32 + lower * 2 + zc

    taps = long_filter.reshape(group, devices, tokens)
    taps, biases, _ = lax.optimization_barrier((taps, biases, odd))
    taps, near, crossed = lax.optimization_barrier((taps, near, crossed))
    moved = [(source, exchanged(source)) for source in range(devices) if exchanged(source) != source]
    swapped = lax.ppermute(taps, ALL, moved)

    near_blocks = (near, crossed, mine, sibling)
    out_second, gated = attend(1, core, biases[1], q_proj, pre_gate, exchanged_half, near_blocks, group)
    out_first, gated = attend(
        0, core, biases[0], q_proj, pre_gate, exchanged_half, (*near_blocks, far), group, gated
    )
    gated, swapped = lax.optimization_barrier((gated, swapped))
    taps = jnp.where(lax.axis_index("zc") == core, taps, swapped)
    spectrum = transform_filter(taps, tables)
    gathered = lax.all_to_all(gated, CHIPS, split_axis=0, concat_axis=0, tiled=True)
    out_mine = jnp.where(first_core, out_first, out_second)
    out_other = to_sibling(jnp.where(first_core, out_second, out_first))
    attn_out = jnp.stack(
        [
            jnp.where(first_core, out_mine, out_other).reshape(STEPS, -1, tokens),
            jnp.where(first_core, out_other, out_mine).reshape(STEPS, -1, tokens),
        ],
        axis=1,
    ).reshape(channels, tokens)

    conv_out = convolve(gathered.reshape(devices, group, tokens), spectrum, tables)
    returned = lax.all_to_all(
        conv_out, OWNERS, split_axis=0, concat_axis=0, tiled=True
    ).reshape(channels, tokens)
    mixed = (post_gate.astype(jnp.float32) * returned.astype(jnp.float32)).astype(jnp.bfloat16)
    return (attn_out, mixed)


def solution(mesh):
    chips = Mesh(mesh.devices.reshape(2, 2, 2, 4, 4, 2), ALL)
    return jax.shard_map(
        body,
        mesh=chips,
        in_specs=(
            P(None, ALL),
            P(None, ALL),
            P(None, ALL),
            P(),
            P(ALL, None),
            P(None, ALL),
            P(None, ALL),
            P(ALL, None),
        ),
        out_specs=(P(None, ALL), P(None, ALL)),
        check_vma=False,
    )
```

```python
import functools
import math

import jax
import jax.numpy as jnp
import ml_dtypes
import numpy as np
from jax import lax
from jax.experimental import pallas as pl
from jax.experimental.pallas import tpu as pltpu
from jax.sharding import Mesh
from jax.sharding import PartitionSpec as P

HD = 128
ALL = ("za", "zb", "zc", "x", "y", "c")
CHIPS = ("za", "zb", "x", "y", "zc")
OWNERS = ("za", "zb", "c", "x", "y", "zc")
STEPS = 4
MASKED = -1e30
VMEM_LIMIT = 48 * 1024 * 1024
HBM_ONLY = 63 * 1024 * 1024


def hi_lo(table):
    high = table.astype(ml_dtypes.bfloat16)
    low = (table - high.astype(np.float64)).astype(ml_dtypes.bfloat16)
    return (high, low)


def make_tables(rows, width):
    length = rows * width
    k1 = np.arange(rows)[:, None]
    n1 = np.arange(rows)[None, :]
    theta = 2.0 * np.pi * (((4 * k1 + 1) * n1) % (4 * rows)) / (4 * rows)
    n2 = np.arange(width)[None, :]
    turn = 2.0 * np.pi * (((4 * k1 + 1) * n2) % (4 * length)) / (4 * length)
    k2 = np.arange(width)[:, None]
    phi = 2.0 * np.pi * ((k2 * n2) % width) / width
    first = hi_lo(np.concatenate([np.cos(theta), -np.sin(theta)], axis=0))
    second = hi_lo(np.block([[np.cos(phi), -np.sin(phi)], [np.sin(phi), np.cos(phi)]]))
    second_back = hi_lo(np.block([[np.cos(phi), np.sin(phi)], [-np.sin(phi), np.cos(phi)]]))
    first_back = hi_lo(np.concatenate([np.cos(theta).T, -np.sin(theta).T], axis=1) / length)
    twist = (np.cos(turn).astype(np.float32), -np.sin(turn).astype(np.float32))
    blocks = np.arange(rows).reshape(4, 2, -1, 2)
    arriving = blocks.transpose(0, 2, 1, 3).reshape(-1)
    leaving = blocks.transpose(0, 3, 2, 1).reshape(-1)
    first_moved = np.concatenate([table[:, arriving] for table in first], axis=1)
    first = np.concatenate(first, axis=1)
    second = np.concatenate([second[0], second[0], second[1]], axis=0)
    second_back = np.concatenate([second_back[0], second_back[0], second_back[1]], axis=0)
    high, low = (table[leaving] for table in first_back)
    first_back = np.concatenate([high, high, low], axis=1)
    return first, first_moved, twist, second, second_back, first_back


def dot(left, right):
    return jnp.dot(left, right, preferred_element_type=jnp.float32)


def split(value):
    high = value.astype(jnp.bfloat16)
    low = (value - high.astype(jnp.float32)).astype(jnp.bfloat16)
    return high, low


def turned_by(real, imag, cosine, sine):
    return real * cosine - imag * sine, real * sine + imag * cosine


def interleaved(tasks, lag=1):
    waiting, active, turn = list(tasks), [], 0
    while waiting or active:
        if waiting and turn % lag == 0:
            active.append(waiting.pop(0))
        active = [task for task in active if next(task, None) is not None]
        turn += 1


def forward(signals, first, cosine, sine, second):
    rows, width = signals[0].shape
    signal = jnp.concatenate(signals, axis=1)
    part = dot(first, jnp.concatenate([signal, signal], axis=0))
    yield part
    turned = []
    for channel in range(2):
        lanes = slice(channel * width, (channel + 1) * width)
        turned.append(
            jnp.concatenate(turned_by(part[:rows, lanes], part[rows:, lanes], cosine, sine), axis=1)
        )
    high, low = split(jnp.concatenate(turned, axis=0))
    yield dot(jnp.concatenate([high, low, high], axis=1), second)


def filter_task(pair, filter_ref, first, cosine, sine, second, out_ref):
    signals = [filter_ref[2 * pair], filter_ref[2 * pair + 1]]
    rows = signals[0].shape[0]
    for spectrum in forward(signals, first[...], cosine[...], sine[...], second[...]):
        yield True
    out_ref[2 * rows * pair : 2 * rows * (pair + 1)] = spectrum


def filter_kernel(filter_ref, *rest):
    pairs = filter_ref.shape[0] // 2
    interleaved([filter_task(pair, filter_ref, *rest) for pair in range(pairs)])


def conv_task(
    channel, place, rows, load, store, spectrum_ref, first, cosine_ref, sine_ref, second, second_back, first_back
):
    width = cosine_ref.shape[1]
    cosine, sine = cosine_ref[...], sine_ref[...]
    signals = [load(channel), load(channel + 1)]
    for spectrum in forward(signals, first[...], cosine, sine, second[...]):
        yield True
    other = spectrum_ref[rows * place : rows * (place + 2)]
    product = jnp.concatenate(
        turned_by(spectrum[:, :width], spectrum[:, width:], other[:, :width], other[:, width:]),
        axis=1,
    )
    high, low = split(product)
    part = dot(jnp.concatenate([high, low, high], axis=1), second_back[...])
    yield True
    reals, imags = [], []
    for half in range(2):
        block = part[half * rows : (half + 1) * rows]
        real, imag = turned_by(block[:, :width], block[:, width:], cosine, -sine)
        reals.append(real)
        imags.append(imag)
    turned = jnp.concatenate(
        [jnp.concatenate(reals, axis=1), jnp.concatenate(imags, axis=1)], axis=0
    )
    high, low = split(turned)
    result = dot(first_back[...], jnp.concatenate([high, low, high], axis=0))
    yield True
    store(channel, result[:, :width])
    store(channel + 1, result[:, width:])


def conv_kernel(signal_ref, spectrum_ref, *rest):
    *tables, out_ref, taken, given = rest
    rows, channels, width = signal_ref.shape
    here = spectrum_ref.shape[0] // rows
    step = pl.program_id(0)
    base = step * here

    @pl.when(step == 0)
    def _():
        taken[...] = signal_ref[...].astype(jnp.float32).reshape(taken.shape)

    def load(channel):
        return taken[pl.ds(base + channel, rows, stride=channels), :].astype(jnp.bfloat16)

    def store(channel, value):
        given[pl.ds(base + channel, rows, stride=channels), :] = value

    interleaved(
        [
            conv_task(channel, channel, rows, load, store, spectrum_ref, *tables)
            for channel in range(0, here, 2)
        ]
    )

    @pl.when(step == pl.num_programs(0) - 1)
    def _():
        out_ref[...] = given[...].reshape(out_ref.shape).astype(jnp.bfloat16)


def whole(array):
    return pl.BlockSpec(array.shape, lambda step: (0,) * array.ndim)


def transform_filter(taps, tables, step_channels=4):
    first, _, twist, second, _, _ = tables
    channels, rows, width = taps.shape
    constants = [jnp.asarray(entry) for entry in (first, *twist, second)]
    return pl.pallas_call(
        filter_kernel,
        grid=(channels // step_channels,),
        in_specs=[pl.BlockSpec((step_channels, rows, width), lambda step: (step, 0, 0))]
        + [whole(entry) for entry in constants],
        out_specs=pl.BlockSpec((step_channels * rows, 2 * width), lambda step: (step, 0)),
        out_shape=jax.ShapeDtypeStruct((channels * rows, 2 * width), jnp.float32),
        compiler_params=pltpu.CompilerParams(vmem_limit_bytes=HBM_ONLY),
        cost_estimate=pl.CostEstimate(
            flops=channels * 170_000_000, bytes_accessed=6 * 1024 * 1024, transcendentals=0
        ),
        name="filter_spectrum",
    )(taps, *constants)


def convolve(signal, spectrum, tables, step_channels=8):
    _, first, twist, second, second_back, first_back = tables
    rows, channels, width = signal.shape
    constants = [jnp.asarray(entry) for entry in (first, *twist, second, second_back, first_back)]
    return pl.pallas_call(
        conv_kernel,
        grid=(channels // step_channels,),
        in_specs=[
            whole(signal),
            pl.BlockSpec((step_channels * rows, 2 * width), lambda step: (step, 0)),
        ]
        + [whole(entry) for entry in constants],
        out_specs=whole(signal),
        out_shape=jax.ShapeDtypeStruct(signal.shape, jnp.bfloat16),
        scratch_shapes=[pltpu.VMEM((rows * channels, width), jnp.float32)] * 2,
        compiler_params=pltpu.CompilerParams(vmem_limit_bytes=HBM_ONLY),
        cost_estimate=pl.CostEstimate(
            flops=channels * 370_000_000, bytes_accessed=8 * 1024 * 1024, transcendentals=0
        ),
        name="convolve",
    )(signal, spectrum, *constants)


def pick_heads(which, first, second):
    tokens = first.shape[1]
    pairs = [value.reshape(STEPS, 2, -1, tokens) for value in (first, second)]
    return jnp.stack(
        [
            lax.dynamic_index_in_dim(pair, which, 1, keepdims=False).reshape(-1, tokens)
            for pair in pairs
        ]
    )


def attend_kernel(
    parity, core_ref, bias_ref, q_mine, gate_mine, q_other, gate_other, near, crossed, own, sibling, *rest
):
    out_ref, gated = rest[-2:]
    heads, tokens = gate_other.shape[0] // HD, gate_other.shape[1]
    group = gated.shape[1]
    is_mine = core_ref[0] == parity
    part_heads = q_mine.shape[1] // HD

    def rows_of(head):
        return slice(head * HD, (head + 1) * HD)

    def chosen(mine_ref, other_ref, head):
        mine = mine_ref[head // part_heads, rows_of(head % part_heads)]
        return jnp.where(is_mine, mine, other_ref[rows_of(head)])

    def window(kind, rows):
        shared = [near[kind, rows], crossed[kind, rows]]
        if parity == 1:
            return jnp.concatenate(shared + [own[kind, rows], sibling[kind, rows]], axis=1)
        itself = jnp.where(is_mine, own[kind, rows], sibling[kind, rows])
        return jnp.concatenate(shared + [rest[0][kind, rows], itself], axis=1)

    def task(head):
        rows = rows_of(head)
        scores = lax.dot_general(
            window(0, rows),
            chosen(q_mine, q_other, head),
            (((0,), (0,)), ((), ())),
            preferred_element_type=jnp.float32,
        )
        yield True
        masked = scores * (math.log2(math.e) / math.sqrt(HD)) + bias_ref[...]
        weights = jnp.exp2(masked - jnp.max(masked, axis=0, keepdims=True))
        total = jnp.sum(weights, axis=0, keepdims=True)
        weights = weights.astype(jnp.bfloat16)
        yield True
        mixed = (dot(window(1, rows), weights) * (1.0 / total)).astype(jnp.bfloat16)
        out_ref[rows] = mixed
        gate = chosen(gate_mine, gate_other, head)
        product = (mixed.astype(jnp.float32) * gate.astype(jnp.float32)).astype(jnp.bfloat16)
        owners = slice(head * HD // group, (head + 1) * HD // group)
        gated[owners] = product.reshape(HD // group, group, tokens)

    interleaved([task(head) for head in range(heads)])


def attend(parity, core, bias, q_proj, gate, exchanged, blocks, group, gated=None, steps=2):
    channels, tokens = q_proj.shape[0] // 2, q_proj.shape[1]
    step_rows = channels // steps
    halves = [value.reshape(STEPS, 2, channels // STEPS, tokens) for value in (q_proj, gate)]
    half = pl.BlockSpec(
        (STEPS // steps, None, channels // STEPS, tokens), lambda step, core: (step, core[0], 0, 0)
    )
    pair = pl.BlockSpec((2, step_rows, tokens), lambda step, core: (0, step, 0))
    pieces = [
        pl.BlockSpec((None, step_rows, tokens), lambda step, core, which=which: (which, step, 0))
        for which in range(2)
    ]
    operands = [core.reshape(1), bias, *halves, exchanged, exchanged, *blocks]
    in_specs = [pl.BlockSpec(bias.shape, lambda step, core: (0, 0)), half, half, *pieces]
    in_specs += [pair] * len(blocks)
    aliases = {}
    if gated is not None:
        aliases = {len(operands): 1}
        operands.append(gated)
        in_specs.append(pl.BlockSpec(memory_space=pl.ANY))
    return pl.pallas_call(
        functools.partial(attend_kernel, parity),
        grid_spec=pltpu.PrefetchScalarGridSpec(
            num_scalar_prefetch=1,
            grid=(steps,),
            in_specs=in_specs,
            out_specs=[
                pl.BlockSpec((step_rows, tokens), lambda step, core: (step, 0)),
                pl.BlockSpec(
                    (step_rows // group, None, group, tokens), lambda step, core: (step, parity, 0, 0)
                ),
            ],
        ),
        out_shape=[
            jax.ShapeDtypeStruct((channels, tokens), jnp.bfloat16),
            jax.ShapeDtypeStruct((channels // group, 2, group, tokens), jnp.bfloat16),
        ],
        input_output_aliases=aliases,
        compiler_params=pltpu.CompilerParams(vmem_limit_bytes=HBM_ONLY),
        cost_estimate=pl.CostEstimate(
            flops=(channels // HD) * 4 * HD * bias.size,
            bytes_accessed=16 * 2 * channels * tokens + 4 * bias.size,
            transcendentals=(channels // HD) * bias.size,
        ),
        name=("attend_first", "attend_second")[parity],
    )(*operands)


def chip_bias(block_start, flags, key_ids, query_ids, tokens):
    opened = (block_start < tokens).astype(jnp.int32)
    all_ids = jnp.arange(block_start.shape[0], dtype=jnp.int32)
    lanes = jnp.arange(tokens, dtype=jnp.int32)

    def records(ids):
        base = jnp.sum(jnp.where(all_ids[None, :] < ids[:, None], opened[None, :], 0), axis=1)
        start = jnp.sum(
            jnp.where(all_ids[None, :] == ids[:, None], block_start[None, :], 0), axis=1
        )
        return base[:, None] + (lanes[None, :] >= start[:, None]).astype(jnp.int32)

    same = records(key_ids)[:, :, None, None] == records(query_ids)[None, None, :, :]
    causal = lanes[None, :, None, None] <= lanes[None, None, None, :]
    distance = query_ids[None, :] - key_ids[:, None]
    picked = jnp.zeros(distance.shape, jnp.int32)
    for step in range(flags.shape[1]):
        picked = jnp.where(distance == step + 1, flags[None, :, step], picked)
    earlier = ((picked == 1) & (key_ids[:, None] >= 0))[:, None, :, None]
    own = (distance == 0)[:, None, :, None]
    visible = same & (earlier | (own & causal))
    bias = jnp.where(visible, 0.0, MASKED).astype(jnp.float32)
    return bias.reshape(key_ids.shape[0] * tokens, query_ids.shape[0] * tokens)


def devices_of():
    return math.prod(lax.axis_size(name) for name in ALL)


def send(value, target):
    count = devices_of()
    return lax.ppermute(value, ALL, [(source, target(source) % count) for source in range(count)])


def next_chip(value):
    return send(value, lambda source: source + 2)


def next_chip_crossed(value):
    return send(value, lambda source: (source + 2) ^ 1)


def second_next_chip(value):
    count, ring = devices_of(), lax.axis_size("y")

    def between(source):
        y = source // 2 % ring
        return source + 2 * ((y - 1) % ring - y)

    value = lax.ppermute(value, "y", [(y, (y - 1) % ring) for y in range(ring)])
    return lax.ppermute(
        value, ALL, [(between(source), (source + 4) % count) for source in range(count)]
    )


def to_sibling(value):
    return lax.ppermute(value, "c", [(0, 1), (1, 0)])


def body(q_proj, k_proj, v_proj, block_start, kv_select, pre_gate, post_gate, long_filter):
    channels, tokens = q_proj.shape
    devices = devices_of()
    group = channels // devices
    tables = make_tables(devices, tokens)
    core = lax.axis_index("c")
    first_core = core == 0

    other = pick_heads(1 - core, k_proj, v_proj)
    sibling = to_sibling(other)
    crossed = next_chip_crossed(other)
    k_later, v_later, other = lax.optimization_barrier((k_proj, v_proj, other))
    mine = pick_heads(core, k_later, v_later)
    near = next_chip(mine)
    odd = jnp.where(first_core, sibling, mine)
    starts, picked, odd = lax.optimization_barrier((block_start, kv_select, odd))
    far = second_next_chip(odd)
    flags = picked.astype(jnp.float32)
    flags = jnp.concatenate([flags, to_sibling(flags)], axis=0).astype(jnp.int32)
    first = 2 * lax.axis_index(ALL[:-1])
    near_ids = [first - 2 + core, first - 1 - core]
    windows = [[first - 3, first], [first + core, first + 1 - core]]
    biases = [
        chip_bias(
            starts,
            jnp.where(core == parity, flags[:1], flags[1:]),
            jnp.stack(near_ids + windows[parity]),
            jnp.stack([first + parity]),
            tokens,
        )
        for parity in range(2)
    ]

    q_later, gate_later, biases, _ = lax.optimization_barrier((q_proj, pre_gate, biases, odd))
    exchanged_half = to_sibling(pick_heads(1 - core, q_later, gate_later))

    def exchanged(source):
        upper, zc, lower, c = source // 64, source // 32 % 2, source // 2 % 16, source % 2
        return upper * 64 + c * 32 + lower * 2 + zc

    taps = long_filter.reshape(group, devices, tokens)
    taps, biases, _ = lax.optimization_barrier((taps, biases, odd))
    taps, near, crossed = lax.optimization_barrier((taps, near, crossed))
    moved = [(source, exchanged(source)) for source in range(devices) if exchanged(source) != source]
    swapped = lax.ppermute(taps, ALL, moved)

    near_blocks = (near, crossed, mine, sibling)
    out_second, gated = attend(1, core, biases[1], q_proj, pre_gate, exchanged_half, near_blocks, group)
    out_first, gated = attend(
        0, core, biases[0], q_proj, pre_gate, exchanged_half, (*near_blocks, far), group, gated
    )
    gated, swapped = lax.optimization_barrier((gated, swapped))
    taps = jnp.where(lax.axis_index("zc") == core, taps, swapped)
    spectrum = transform_filter(taps, tables)
    gathered = lax.all_to_all(gated, CHIPS, split_axis=0, concat_axis=0, tiled=True)
    out_mine = jnp.where(first_core, out_first, out_second)
    out_other = to_sibling(jnp.where(first_core, out_second, out_first))
    attn_out = jnp.stack(
        [
            jnp.where(first_core, out_mine, out_other).reshape(STEPS, -1, tokens),
            jnp.where(first_core, out_other, out_mine).reshape(STEPS, -1, tokens),
        ],
        axis=1,
    ).reshape(channels, tokens)

    conv_out = convolve(gathered.reshape(devices, group, tokens), spectrum, tables)
    returned = lax.all_to_all(
        conv_out, OWNERS, split_axis=0, concat_axis=0, tiled=True
    ).reshape(channels, tokens)
    mixed = (post_gate.astype(jnp.float32) * returned.astype(jnp.float32)).astype(jnp.bfloat16)
    return (attn_out, mixed)


def solution(mesh):
    chips = Mesh(mesh.devices.reshape(2, 2, 2, 4, 4, 2), ALL)
    return jax.shard_map(
        body,
        mesh=chips,
        in_specs=(
            P(None, ALL),
            P(None, ALL),
            P(None, ALL),
            P(),
            P(ALL, None),
            P(None, ALL),
            P(None, ALL),
            P(ALL, None),
        ),
        out_specs=(P(None, ALL), P(None, ALL)),
        check_vma=False,
    )
```
